256 devices in a mesh: feed: 128 (over y_lo, x, z, core), rep: 2 (over y_hi).
Axes of the slice: x: 4, y: 4 (y_hi: 2, y_lo: 2; y = y_hi * 2 + y_lo), z: 8, core: 2. Of those that a mesh axis runs over, the one named last changes fastest.
Arguments:
- voltages: bfloat16 [1024, 262144], P('feed', 'rep'), may hold values from -6 to 6
- pfb_window: float32 [8192], replicated, may hold values from 0.1 to 2
- channel_map: int32 [512], replicated, may hold values from 0 to 511, each once
- beam_layout: int32 [1024], replicated, may hold values from 0 to 1023, each once
Outputs:
- visibilities: bfloat16 [512, 1024, 2, 1024], P('rep', 'feed')
- beam_power: float32 [1024, 512], P('feed')
The draws below stay inside these ranges and needn't reach their ends.
Inputs may be any that keep to these rules, and one draw needn't show every extreme that they name: `channel_map`: each channel appears once. `beam_layout`: each input appears once.
All inputs are finite; a program needn't handle non-finite values.
Results may differ from the reference program's by a relative error of at most 0.006.
Values may be sent and summed in bfloat16 or wider, within the bound.
No kernel may reach another device: no remote copies, remote signals or barrier semaphores. Data moves between devices by JAX's collectives and lax.ppermute only.
A program may use at most 192 MiB of HBM per device.

```python
import math
import jax
import jax.numpy as jnp
import numpy as np
from jax import lax

CYL = 4
POS = 128
DFT = 2048
CHANNELS = 512
CH0 = 256
TAPS = 4
INPUTS = 1024
SLOTS = 1024
FRAMES = 128
SAMPLES = 262144


def block_levels(own_key, extent, shards, low, high):
    factor_of = 1.0
    for axis_at, shards_of in shards:
        draws = jax.random.uniform(jax.random.fold_in(jax.random.fold_in(own_key, 6), axis_at), (shards_of,), jnp.float32, low / len(shards), high / len(shards))
        factor_of = factor_of * jnp.repeat(jnp.exp(draws), extent[axis_at] // shards_of).reshape((-1,) + (1,) * (len(extent) - 1 - axis_at))
    return factor_of


def gaussian(key, dims, spread, most, shards=(), held_as=jnp.bfloat16):
    values = jax.random.normal(key, dims, jnp.float32) * spread
    if len(shards) > 0:
        values = block_levels(key, dims, shards, -0.22, 0.18) * values
    return jnp.clip(values, min=-most, max=most).astype(held_as)


def setup_inputs(seed: int = 0) -> dict:
    splits = jax.random.split(jax.random.key(seed), 5)
    voltages = gaussian(splits[0], (INPUTS, SAMPLES), 1.0, 6.0, ((0, 128), (1, 2)))
    pfb_window = jnp.clip(jnp.exp(jax.random.uniform(splits[1], (TAPS * DFT,), jnp.float32, math.log(0.1), math.log(2.0))), 0.1, 2.0)
    channel_map = jax.random.permutation(splits[2], CHANNELS).astype(jnp.int32)
    beam_layout = jax.random.permutation(splits[3], INPUTS).astype(jnp.int32)
    return {"voltages": voltages, "pfb_window": pfb_window, "channel_map": channel_map, "beam_layout": beam_layout}


def wave_columns(dft_length, channels, first_bin):
    samples = jnp.arange(dft_length, dtype=jnp.int32)
    freq_bins = jnp.arange(channels, dtype=jnp.int32) + first_bin
    phase_index = samples[:, None] * freq_bins[None, :] % dft_length
    angles = phase_index.astype(jnp.float32) * (2.0 * np.pi / dft_length)
    return jnp.concatenate([jnp.cos(angles), -jnp.sin(angles)], axis=1)

def weight_taps(window_part, wave_table, tap_count, norm_taps, channels):
    dft_length = wave_table.shape[0]
    weighted = window_part.reshape(tap_count, dft_length, 1) * wave_table[None] / math.sqrt(norm_taps * channels)
    return weighted.astype(jnp.bfloat16)

def position_tables(grid_size):
    places = jnp.arange(grid_size, dtype=jnp.int32)
    phase_index = places[:, None] * places[None, :] % grid_size
    angles = phase_index.astype(jnp.float32) * (2.0 * np.pi / grid_size)
    return jnp.stack([jnp.cos(angles), jnp.sin(angles)]).astype(jnp.bfloat16)

def quarter_tables(cylinders):
    quarter_turns = np.arange(cylinders)[:, None] * np.arange(cylinders)[None, :] % 4
    real_table = np.array([1.0, 0.0, -1.0, 0.0])[quarter_turns]
    imag_table = np.array([0.0, -1.0, 0.0, 1.0])[quarter_turns]
    return (jnp.asarray(real_table, jnp.float32), jnp.asarray(imag_table, jnp.float32))

def beam_intensity(cell_grid, beam_tables, turn_real, turn_imag, beam_scale):
    highest = lax.Precision.HIGHEST
    mixed = jnp.einsum('anp,cpqf->ancqf', beam_tables, cell_grid, precision=highest)
    north_real = mixed[0, :, :, 0] + mixed[1, :, :, 1]
    north_imag = mixed[0, :, :, 1] - mixed[1, :, :, 0]
    east_real = jnp.einsum('ec,ncf->enf', turn_real, north_real, precision=highest) - jnp.einsum('ec,ncf->enf', turn_imag, north_imag, precision=highest)
    east_imag = jnp.einsum('ec,ncf->enf', turn_imag, north_real, precision=highest) + jnp.einsum('ec,ncf->enf', turn_real, north_imag, precision=highest)
    return lax.optimization_barrier(jnp.sum(east_real * east_real + east_imag * east_imag, axis=2)).reshape(-1) * beam_scale

def reference(voltages, pfb_window, channel_map, beam_layout):
    wave_table = wave_columns(DFT, CHANNELS, CH0)
    fir_table = weight_taps(pfb_window, wave_table, TAPS, TAPS, CHANNELS)
    sample_blocks = voltages.reshape(INPUTS, FRAMES, DFT)
    padded = jnp.concatenate([jnp.zeros((INPUTS, TAPS - 1, DFT), voltages.dtype), sample_blocks], axis=1)
    grouped = padded.reshape(INPUTS // 32, 32, FRAMES + TAPS - 1, DFT)

    def filter_group(group_data):
        running = jnp.zeros((32, SLOTS, FRAMES), jnp.float32)
        for tap_index in range(TAPS):
            running = running + jnp.einsum('ifk,km->imf', group_data[:, tap_index:tap_index + FRAMES].astype(jnp.float32), fir_table[tap_index].astype(jnp.float32))
        return running.astype(jnp.bfloat16)
    spectra = lax.map(filter_group, grouped).reshape(INPUTS, SLOTS, FRAMES)
    beam_tables = position_tables(POS).astype(jnp.float32)
    turn_real, turn_imag = quarter_tables(CYL)
    beam_scale = 1.0 / (FRAMES * CYL * POS)

    def one_slot(slot_index):
        channel = channel_map[slot_index // 2]
        half_index = slot_index % 2
        real_rows = jnp.take(spectra, channel, axis=1)
        imag_rows = jnp.take(spectra, channel + CHANNELS, axis=1)
        both_parts = jnp.stack([real_rows, imag_rows], axis=1)
        own_rows = lax.dynamic_slice_in_dim(both_parts, half_index * (INPUTS // 2), INPUTS // 2, 0)
        real_part = jnp.dot(own_rows[:, 0], real_rows.T, preferred_element_type=jnp.float32) + jnp.dot(own_rows[:, 1], imag_rows.T, preferred_element_type=jnp.float32)
        imag_part = jnp.dot(own_rows[:, 1], real_rows.T, preferred_element_type=jnp.float32) - jnp.dot(own_rows[:, 0], imag_rows.T, preferred_element_type=jnp.float32)
        visible = (jnp.stack([real_part, imag_part], axis=1) / FRAMES).astype(jnp.bfloat16)
        row_order = lax.dynamic_slice_in_dim(beam_layout, half_index * (CYL * POS), CYL * POS)
        cell_grid = jnp.take(both_parts, row_order, axis=0).reshape(CYL, POS, 2, FRAMES)
        power = beam_intensity(cell_grid.astype(jnp.float32), beam_tables, turn_real, turn_imag, beam_scale)
        return (visible, power)
    slot_ids = jnp.arange(SLOTS, dtype=jnp.int32)
    visible_all, power_all = lax.map(one_slot, slot_ids)
    return (jnp.transpose(visible_all, (1, 0, 2, 3)), power_all)
```

```python
import math

import jax
import jax.numpy as jnp
import numpy as np
from jax import lax
from jax.experimental import pallas as pl
from jax.experimental.pallas import tpu as pltpu
from jax.sharding import PartitionSpec as P

CYL = 4
POS = 128
DFT = 2048
CHANNELS = 512
CH0 = 256
TAPS = 4
HALF = DFT // 2
VMEM = 56 * 1024 * 1024
NT = (((1,), (1,)), ((), ()))


def wave_rows():
    samples = np.arange(HALF)
    rows = []
    for parity in range(2):
        bins = CH0 + np.arange(parity, CHANNELS, 2)
        angles = (bins[:, None] * samples[None, :] % DFT) * (2.0 * np.pi / DFT)
        rows += [np.cos(angles), -np.sin(angles)]
    return np.concatenate(rows).astype(np.float32).astype(jnp.bfloat16)


def order_table(inputs, frames):
    part, frame, feed = np.meshgrid(
        np.arange(2), np.arange(frames), np.arange(inputs), indexing="ij"
    )
    target = ((feed * 2 + part) * frames + frame).reshape(-1)
    table = np.zeros((target.size, target.size), np.float32)
    table[np.arange(target.size), target] = 1.0
    return table.astype(jnp.bfloat16)


def position_tables():
    places = np.arange(POS)
    angles = (places[:, None] * places[None, :] % POS) * (2.0 * np.pi / POS)
    tables = np.concatenate([np.cos(angles), np.sin(angles)])
    return tables.astype(np.float32).astype(jnp.bfloat16)


def filter_kernel(volt, margin, window, waves, order, slots, out, blocks, spectra, sorted_, rows):
    inputs = volt.shape[0]
    frames = volt.shape[1] // DFT
    scale = 1.0 / math.sqrt(TAPS * CHANNELS)

    def taps_of(at):
        return [window[:, pl.ds(t * DFT + at, 128)] * scale for t in range(TAPS)]

    def chunk(j, carry):
        low = pl.multiple_of(j * 128, 128)
        high = pl.multiple_of(j * 128 + HALF, 128)
        sums = []
        for at in (low, high):
            weights = [jnp.broadcast_to(w, (inputs, 128)) for w in taps_of(at)]
            held = [margin[:, pl.ds(t * DFT + at, 128)].astype(jnp.float32) for t in range(3)]
            column = []
            for f in range(frames):
                held.append(volt[:, pl.ds(f * DFT + at, 128)].astype(jnp.float32))
                total = held[0] * weights[0]
                for t in range(1, TAPS):
                    total = total + held[t] * weights[t]
                held = held[1:]
                column.append(total)
            sums.append(column)
        for f in range(0, frames, 2):
            for parity in range(2):
                pair = []
                for g in (f, f + 1):
                    first, second = sums[0][g], sums[1][g]
                    pair.append(first - second if parity else first + second)
                blocks[parity, pl.ds(f * inputs, 2 * inputs), pl.ds(low, 128)] = jnp.concatenate(
                    pair, axis=0
                ).astype(jnp.bfloat16)
        return carry

    lax.fori_loop(0, HALF // 128, chunk, 0)

    columns = inputs * frames
    half_ch = CHANNELS // 2
    for parity in range(2):
        for part in range(2):
            first = (parity * 2 + part) * half_ch
            spectra[parity * half_ch : (parity + 1) * half_ch, part * columns : (part + 1) * columns] = (
                lax.dot_general(
                    waves[first : first + half_ch, :],
                    blocks[parity],
                    NT,
                    preferred_element_type=jnp.float32,
                ).astype(jnp.bfloat16)
            )
    for at in range(0, 2 * columns, 256):
        sorted_[:, at : at + 256] = jnp.dot(
            spectra[...], order[:, at : at + 256], preferred_element_type=jnp.float32
        ).astype(jnp.bfloat16)
    place = lax.broadcasted_iota(jnp.int32, (slots.shape[0], CHANNELS), 1)
    channel = jnp.where(place < half_ch, 2 * place, 2 * (place - half_ch) + 1)
    wide = 2 * frames
    for c in range(slots.shape[1]):
        pick = (channel == slots[:, c : c + 1]).astype(jnp.float32).astype(jnp.bfloat16)
        for pair in range(0, inputs, 2):
            picked = jnp.dot(
                pick,
                sorted_[:, pair * wide : (pair + 2) * wide],
                preferred_element_type=jnp.float32,
            )
            for i in range(2):
                rows[pl.ds(pair + i, slots.shape[0], stride=inputs), :] = picked[
                    :, i * wide : (i + 1) * wide
                ]
        out[:, c * wide : (c + 1) * wide] = rows[...].astype(jnp.bfloat16)


def filtered(volt, margin, window, slots):
    inputs, own = volt.shape
    frames = own // DFT
    dests, chans = slots.shape
    columns = inputs * frames
    return pl.pallas_call(
        filter_kernel,
        out_shape=jax.ShapeDtypeStruct((dests * inputs, chans * 2 * frames), jnp.bfloat16),
        scratch_shapes=[
            pltpu.VMEM((2, columns, HALF), jnp.bfloat16),
            pltpu.VMEM((CHANNELS, 2 * columns), jnp.bfloat16),
            pltpu.VMEM((CHANNELS, 2 * columns), jnp.bfloat16),
            pltpu.VMEM((dests * inputs, 2 * frames), jnp.float32),
        ],
        compiler_params=pltpu.CompilerParams(vmem_limit_bytes=VMEM),
        cost_estimate=pl.CostEstimate(
            flops=2 * columns * CHANNELS * 5 * 1024, bytes_accessed=8 << 20, transcendentals=0
        ),
        name="polyphase",
    )(volt, margin, window, wave_rows(), order_table(inputs, frames), slots)


def beam_kernel(scale, own, layout, tables, out, mixer, mixed):
    inputs = own.shape[0]
    chans = own.shape[1] // 128
    half = CYL * POS
    lane = lax.broadcasted_iota(jnp.int32, (POS, 128), 1)
    first = lane < 64
    collected = jnp.zeros((POS, 128), jnp.float32)
    feed = lax.broadcasted_iota(jnp.int32, (inputs, POS), 0)
    for h in range(2):
        for y in range(CYL):
            at = h * half + y * POS
            hit = (feed == layout[:, at : at + POS]).astype(jnp.float32).astype(jnp.bfloat16)
            mixer[y * 2 * POS : (y + 1) * 2 * POS, :] = lax.dot_general(
                tables[...], hit, NT, preferred_element_type=jnp.float32
            ).astype(jnp.bfloat16)
        mixed[...] = jnp.dot(mixer[...], own[...], preferred_element_type=jnp.float32)

        def turned(value):
            other = pltpu.roll(value, 64, 1)
            return jnp.where(first, other, -other)

        for c in range(chans):
            at = c * 128
            north = []
            for y in range(CYL):
                base = y * 2 * POS
                cosine = mixed[base : base + POS, at : at + 128]
                sine = mixed[base + POS : base + 2 * POS, at : at + 128]
                north.append(cosine + turned(sine))
            even, odd = north[0] + north[2], north[1] + north[3]
            gap, step = north[0] - north[2], turned(north[1] - north[3])
            easts = [even + odd, gap + step, even - odd, gap - step]
            for e, east in enumerate(easts):
                power = jnp.sum(east * east, axis=1, keepdims=True)
                collected = jnp.where(lane == e * 2 * chans + c * 2 + h, power, collected)
    turned_over = collected.T
    for e in range(CYL):
        out[:, e * POS : (e + 1) * POS] = turned_over[e * 2 * chans : (e + 1) * 2 * chans, :] * scale


def beams(own, layout, scale):
    inputs, wide = own.shape
    chans = wide // 128
    return pl.pallas_call(
        lambda *refs: beam_kernel(scale, *refs),
        out_shape=jax.ShapeDtypeStruct((2 * chans, CYL * POS), jnp.float32),
        scratch_shapes=[
            pltpu.VMEM((CYL * 2 * POS, inputs), jnp.bfloat16),
            pltpu.VMEM((CYL * 2 * POS, wide), jnp.float32),
        ],
        compiler_params=pltpu.CompilerParams(vmem_limit_bytes=VMEM),
        cost_estimate=pl.CostEstimate(
            flops=4 * 1024 * inputs * wide, bytes_accessed=4 << 20, transcendentals=0
        ),
        name="beams",
    )(own, layout, position_tables())


def gram_kernel(scale, rep, own, other, beam_own, beam_other, out, beam, rows):
    step = pl.program_id(0)
    count = out.shape[0]
    inputs = own.shape[0]

    @pl.when(step == 0)
    def _():
        beam[...] = beam_own[...] + beam_other[...]

    start = pl.multiple_of((step % 2) * (inputs // 2) + rep[0] * count, count)
    lane = lax.broadcasted_iota(jnp.int32, (count, 128), 1)
    plain, turned = [], []
    for source in (own, other):
        part = source[pl.ds(start, count), :]
        plain.append(part)
        swapped = pltpu.roll(part.astype(jnp.float32), 64, 1)
        turned.append(jnp.where(lane < 64, swapped, -swapped).astype(jnp.bfloat16))
    left = jnp.concatenate(
        [jnp.concatenate(plain, axis=1), jnp.concatenate(turned, axis=1)], axis=0
    )
    for at in range(0, inputs, 256):
        right = jnp.concatenate([own[at : at + 256, :], other[at : at + 256, :]], axis=1)
        products = lax.dot_general(left, right, NT, preferred_element_type=jnp.float32)
        for tile in range(2):
            for part in range(2):
                rows[pl.ds((at // 128 + tile) * 2 + part, count, stride=inputs // 64), :] = products[
                    part * count : (part + 1) * count, tile * 128 : (tile + 1) * 128
                ]
    out[:, 0] = (rows[...] * scale).astype(jnp.bfloat16).reshape(count, inputs // 64, 128)


def gram(rep, own, other, beam_own, beam_other, count, total_frames):
    inputs, wide = own.shape
    slots = 2 * (wide // 128)
    spec = pl.BlockSpec((inputs, 128), lambda s: (0, s // 2))
    small = pl.BlockSpec(beam_own.shape, lambda s: (0, 0))
    return pl.pallas_call(
        lambda *refs: gram_kernel(1.0 / total_frames, *refs),
        grid=(slots,),
        in_specs=[pl.BlockSpec(memory_space=pltpu.SMEM), spec, spec, small, small],
        out_specs=[
            pl.BlockSpec((count, 1, inputs // 64, 128), lambda s: (0, s, 0, 0)),
            small,
        ],
        out_shape=[
            jax.ShapeDtypeStruct((count, slots, inputs // 64, 128), jnp.bfloat16),
            jax.ShapeDtypeStruct(beam_own.shape, jnp.float32),
        ],
        scratch_shapes=[pltpu.VMEM((count * (inputs // 64), 128), jnp.float32)],
        compiler_params=pltpu.CompilerParams(vmem_limit_bytes=VMEM),
        cost_estimate=pl.CostEstimate(
            flops=4 * slots * count * inputs * 256, bytes_accessed=12 << 20, transcendentals=0
        ),
        name="gram",
    )(rep, own, other, beam_own, beam_other)


def on_device(voltages, pfb_window, channel_map, beam_layout):
    feed_count = lax.axis_size("feed")
    rep_count = lax.axis_size("rep")
    inp_dev, own_samples = voltages.shape
    total_frames = own_samples // DFT * rep_count
    inputs = inp_dev * feed_count
    swap = [(0, 1), (1, 0)]
    margin = lax.ppermute(voltages[:, own_samples - (TAPS - 1) * DFT :], "rep", [(0, 1)])
    outgoing = filtered(
        voltages, margin, pfb_window.reshape(1, -1), channel_map.reshape(feed_count, -1)
    )
    own = lax.all_to_all(outgoing, "feed", split_axis=0, concat_axis=0, tiled=True)
    other = lax.ppermute(own, "rep", swap)
    beam_own = beams(own, beam_layout.reshape(1, -1), 1.0 / (total_frames * CYL * POS))
    beam_other = lax.ppermute(beam_own, "rep", swap)
    rep = lax.axis_index("rep").reshape(1)
    count = inputs // 2 // rep_count
    summed, beam_power = gram(rep, own, other, beam_own, beam_other, count, total_frames)
    tiles = inputs // 128
    visibilities = summed.reshape(count, -1, tiles, 2, 128).transpose(0, 1, 3, 2, 4)
    return visibilities.reshape(count, -1, 2, inputs), beam_power


def solution(mesh):
    return jax.shard_map(
        on_device,
        mesh=mesh,
        in_specs=(P("feed", "rep"), P(), P(), P()),
        out_specs=(P("rep", "feed", None, None), P("feed", None)),
        check_vma=False,
    )
```

```python
import math

import jax
import jax.numpy as jnp
import numpy as np
from jax import lax
from jax.experimental import pallas as pl
from jax.experimental.pallas import tpu as pltpu
from jax.sharding import PartitionSpec as P

CYL = 4
POS = 128
DFT = 2048
CHANNELS = 512
CH0 = 256
TAPS = 4
HALF = DFT // 2
VMEM = 24 * 1024 * 1024
GROUPS = 4
PARTS = (2, 1, 1)
NT = (((1,), (1,)), ((), ()))


def wave_columns():
    samples = np.arange(HALF)
    tables = []
    for parity in range(2):
        bins = CH0 + np.arange(parity, CHANNELS, 2)
        angles = (samples[:, None] * bins[None, :] % DFT) * (2.0 * np.pi / DFT)
        tables.append(np.concatenate([np.cos(angles), -np.sin(angles)], axis=1))
    return np.stack(tables).astype(np.float32).astype(jnp.bfloat16)


def order_table(inputs, frames):
    frame, feed = np.meshgrid(np.arange(frames), np.arange(inputs), indexing="ij")
    target = (feed * frames + frame).reshape(-1)
    table = np.zeros((target.size, target.size), np.float32)
    table[target, np.arange(target.size)] = 1.0
    return table.astype(jnp.bfloat16)


def position_tables():
    places = np.arange(POS)
    angles = (places[:, None] * places[None, :] % POS) * (2.0 * np.pi / POS)
    tables = np.concatenate([np.cos(angles), np.sin(angles)])
    return tables.astype(np.float32).astype(jnp.bfloat16)


def filter_kernel(
    volt_hbm, margin, window_hbm, waves_hbm, order_hbm, slots_hbm, out,
    volt, window, slots, waves, order, blocks, spectra, sorted_, pick, rows, sems,
):
    inputs = volt.shape[0]
    frames = volt.shape[1] // DFT
    dests = out.shape[0] // inputs
    chans = slots.shape[1] // dests
    scale = 1.0 / math.sqrt(TAPS * CHANNELS)
    group = frames // GROUPS
    span = group * DFT
    copies = [
        pltpu.make_async_copy(
            volt_hbm.at[:, pl.ds(g * span, span)], volt.at[:, pl.ds(g * span, span)], sems.at[g]
        )
        for g in range(GROUPS)
    ]
    for parity in range(2):
        copies.append(
            pltpu.make_async_copy(
                waves_hbm.at[parity], waves.at[parity], sems.at[GROUPS + parity]
            )
        )
    copies.append(pltpu.make_async_copy(order_hbm, order, sems.at[GROUPS + 2]))
    taps_copy = pltpu.make_async_copy(window_hbm, window, sems.at[GROUPS + 3])
    taps_copy.start()
    slots_copy = pltpu.make_async_copy(slots_hbm, slots, sems.at[GROUPS + 4])
    slots_copy.start()
    for copy in copies:
        copy.start()

    half_ch = CHANNELS // 2
    place = lax.broadcasted_iota(jnp.int32, (dests, CHANNELS), 1)
    channel = jnp.where(place < half_ch, 2 * place, 2 * (place - half_ch) + 1)
    dest = lax.broadcasted_iota(jnp.int32, (dests, CHANNELS), 0)
    slots_copy.wait()
    held_by = slots[...].astype(jnp.float32)
    for c in range(chans):
        wanted = jnp.sum(
            jnp.where(place == dest * chans + c, held_by, 0.0), axis=1, keepdims=True
        ).astype(jnp.int32)
        pick[c * dests : (c + 1) * dests, :] = (
            (channel == wanted).astype(jnp.float32).astype(jnp.bfloat16)
        )
    taps_copy.wait()

    def fold(g):
        def chunk(j, carry):
            low = pl.multiple_of(j * 128, 128)
            sums = []
            for at in (low, pl.multiple_of(low + HALF, 128)):
                weights = [
                    jnp.broadcast_to(window[:, pl.ds(t * DFT + at, 128)] * scale, (inputs, 128))
                    for t in range(TAPS)
                ]

                def frame(f):
                    if f < 0:
                        value = margin[:, pl.ds((f + TAPS - 1) * DFT + at, 128)]
                    else:
                        value = volt[:, pl.ds(f * DFT + at, 128)]
                    return value.astype(jnp.float32)

                held = [frame(g * group + t + 1 - TAPS) for t in range(TAPS - 1)]
                column = []
                for f in range(g * group, (g + 1) * group):
                    held.append(frame(f))
                    total = held[0] * weights[0]
                    for t in range(1, TAPS):
                        total = total + held[t] * weights[t]
                    held = held[1:]
                    column.append(total)
                sums.append(column)
            for f in range(0, group, 2):
                for parity in range(2):
                    pair = []
                    for k in (f, f + 1):
                        first, second = sums[0][k], sums[1][k]
                        pair.append(first - second if parity else first + second)
                    at = (g * group + f) * inputs
                    blocks[parity, at : at + 2 * inputs, pl.ds(low, 128)] = jnp.concatenate(
                        pair, axis=0
                    ).astype(jnp.bfloat16)
            return carry

        lax.fori_loop(0, HALF // 128, chunk, 0)

    for g in range(GROUPS):
        copies[g].wait()
        fold(g)

    for parity in range(2):
        copies[GROUPS + parity].wait()
        spectra[:, parity * CHANNELS : (parity + 1) * CHANNELS] = jnp.dot(
            blocks[parity], waves[parity], preferred_element_type=jnp.float32
        ).astype(jnp.bfloat16)
    copies[GROUPS + 2].wait()
    for parity in range(2):
        for part in range(2):
            at = parity * CHANNELS + part * half_ch
            turned = jnp.dot(
                order[...], spectra[:, at : at + half_ch], preferred_element_type=jnp.float32
            ).astype(jnp.bfloat16)
            for i in range(inputs):
                to = (2 * i + part) * frames
                sorted_[to : to + frames, parity * half_ch : (parity + 1) * half_ch] = turned[
                    i * frames : (i + 1) * frames, :
                ]
    wide = 2 * frames
    pitch = inputs + 1
    for pair in range(0, inputs, 2):
        picked = lax.dot_general(
            pick[...],
            sorted_[pair * wide : (pair + 2) * wide, :],
            NT,
            preferred_element_type=jnp.float32,
        )
        for c in range(chans):
            for i in range(2):
                rows[pl.ds(c * dests * pitch + pair + i, dests, stride=pitch), :] = picked[
                    c * dests : (c + 1) * dests, i * wide : (i + 1) * wide
                ]
    for c in range(chans):
        for dest in range(0, dests, 2):
            at = (c * dests + dest) * pitch
            pair = [rows[at + k * pitch : at + k * pitch + inputs, :] for k in range(2)]
            out[dest * inputs : (dest + 2) * inputs, c * wide : (c + 1) * wide] = jnp.concatenate(
                pair, axis=0
            ).astype(jnp.bfloat16)


def filtered(volt, margin, window, slots, dests):
    inputs, own = volt.shape
    frames = own // DFT
    chans = slots.shape[1] // dests
    columns = inputs * frames
    vmem = pl.BlockSpec(memory_space=pltpu.VMEM)
    hbm = pl.BlockSpec(memory_space=pltpu.HBM)
    waves, order = jnp.asarray(wave_columns()), jnp.asarray(order_table(inputs, frames))
    volt, window, waves, order, slots = (
        pltpu.with_memory_space_constraint(array, pltpu.HBM)
        for array in (volt, window, waves, order, slots)
    )
    return pl.pallas_call(
        filter_kernel,
        in_specs=[hbm, vmem, hbm, hbm, hbm, hbm],
        out_specs=vmem,
        out_shape=jax.ShapeDtypeStruct((dests * inputs, chans * 2 * frames), jnp.bfloat16),
        scratch_shapes=[
            pltpu.VMEM(volt.shape, jnp.bfloat16),
            pltpu.VMEM(window.shape, jnp.float32),
            pltpu.VMEM(slots.shape, jnp.int32),
            pltpu.VMEM(waves.shape, jnp.bfloat16),
            pltpu.VMEM(order.shape, jnp.bfloat16),
            pltpu.VMEM((2, columns, HALF), jnp.bfloat16),
            pltpu.VMEM((columns, 2 * CHANNELS), jnp.bfloat16),
            pltpu.VMEM((2 * columns, CHANNELS), jnp.bfloat16),
            pltpu.VMEM((chans * dests, CHANNELS), jnp.bfloat16),
            pltpu.VMEM((chans * dests * (inputs + 1), 2 * frames), jnp.float32),
            pltpu.SemaphoreType.DMA((GROUPS + 5,)),
        ],
        compiler_params=pltpu.CompilerParams(vmem_limit_bytes=VMEM),
        cost_estimate=pl.CostEstimate(
            flops=2 * columns * CHANNELS * 4 * 1024, bytes_accessed=8 << 20, transcendentals=0
        ),
        name="polyphase",
    )(volt, margin, window, waves, order, slots)


def beam_kernel(scale, own, layout, tables, out, mixer, mixed):
    inputs = own.shape[0]
    chans = own.shape[1] // 128
    half = CYL * POS
    lane = lax.broadcasted_iota(jnp.int32, (POS, 128), 1)
    first = lane < 64
    collected = jnp.zeros((POS, 128), jnp.float32)
    feed = lax.broadcasted_iota(jnp.int32, (inputs, POS), 0)
    for h in range(2):
        for y in range(CYL):
            at = h * half + y * POS
            hit = (feed == layout[:, at : at + POS]).astype(jnp.float32).astype(jnp.bfloat16)
            mixer[y * 2 * POS : (y + 1) * 2 * POS, :] = lax.dot_general(
                tables[...], hit, NT, preferred_element_type=jnp.float32
            ).astype(jnp.bfloat16)
        mixed[...] = jnp.dot(mixer[...], own[...], preferred_element_type=jnp.float32)

        def turned(value):
            other = pltpu.roll(value, 64, 1)
            return jnp.where(first, other, -other)

        for c in range(chans):
            at = c * 128
            north = []
            for y in range(CYL):
                base = y * 2 * POS
                cosine = mixed[base : base + POS, at : at + 128]
                sine = mixed[base + POS : base + 2 * POS, at : at + 128]
                north.append(cosine + turned(sine))
            even, odd = north[0] + north[2], north[1] + north[3]
            gap, step = north[0] - north[2], turned(north[1] - north[3])
            easts = [even + odd, gap + step, even - odd, gap - step]
            for e, east in enumerate(easts):
                power = jnp.sum(east * east, axis=1, keepdims=True)
                collected = jnp.where(lane == e * 2 * chans + c * 2 + h, power, collected)
    turned_over = collected.T
    for e in range(CYL):
        out[:, e * POS : (e + 1) * POS] = turned_over[e * 2 * chans : (e + 1) * 2 * chans, :] * scale


def beams(own, layout, scale):
    inputs, wide = own.shape
    chans = wide // 128
    return pl.pallas_call(
        lambda *refs: beam_kernel(scale, *refs),
        out_shape=jax.ShapeDtypeStruct((2 * chans, CYL * POS), jnp.float32),
        scratch_shapes=[
            pltpu.VMEM((CYL * 2 * POS, inputs), jnp.bfloat16),
            pltpu.VMEM((CYL * 2 * POS, wide), jnp.float32),
        ],
        compiler_params=pltpu.CompilerParams(vmem_limit_bytes=VMEM),
        cost_estimate=pl.CostEstimate(
            flops=4 * 1024 * inputs * wide, bytes_accessed=4 << 20, transcendentals=0
        ),
        name="beams",
    )(own, layout, position_tables())


def gram_kernel(scale, rep, own, other, *refs):
    out, rows = refs[-2:]
    if len(refs) > 3:
        beam_own, beam_other, out, beam, rows = refs[-5:]
        beam[...] = beam_own[...] + beam_other[...]
    step = pl.program_id(0)
    count, _, tiles, _ = out.shape
    inputs = own.shape[0]
    pitch = tiles + 1
    start = pl.multiple_of((step % 2) * (inputs // 2) + rep[0] * count, count)
    lane = lax.broadcasted_iota(jnp.int32, (count, 128), 1)
    plain, turned = [], []
    for source in (own, other):
        part = source[pl.ds(start, count), :]
        plain.append(part)
        swapped = pltpu.roll(part.astype(jnp.float32), 64, 1)
        turned.append(jnp.where(lane < 64, swapped, -swapped).astype(jnp.bfloat16))
    left = jnp.concatenate(
        [jnp.concatenate(plain, axis=1), jnp.concatenate(turned, axis=1)], axis=0
    )
    for at in range(0, inputs, 256):
        right = jnp.concatenate([own[at : at + 256, :], other[at : at + 256, :]], axis=1)
        products = lax.dot_general(left, right, NT, preferred_element_type=jnp.float32)
        for tile in range(2):
            for part in range(2):
                rows[pl.ds((at // 128 + tile) * 2 + part, count, stride=pitch), :] = products[
                    part * count : (part + 1) * count, tile * 128 : (tile + 1) * 128
                ]
    for r in range(count):
        out[r, 0] = (rows[r * pitch : r * pitch + tiles, :] * scale).astype(jnp.bfloat16)


def gram(rep, own, other, first, extra, count, total_frames):
    inputs, wide = own.shape
    slots = 2 * (wide // 128)
    steps = 2 * (other.shape[1] // 128)
    tiles = inputs // 64
    ops = [rep, own, other, *extra]
    specs = [
        pl.BlockSpec(memory_space=pltpu.SMEM),
        pl.BlockSpec((inputs, 128), lambda s: (0, first + s // 2)),
        pl.BlockSpec((inputs, 128), lambda s: (0, s // 2)),
    ]
    out_specs = [pl.BlockSpec((count, 1, tiles, 128), lambda s: (0, s + 2 * first, 0, 0))]
    out_shape = [jax.ShapeDtypeStruct((count, slots, tiles, 128), jnp.bfloat16)]
    if extra:
        specs.append(pl.BlockSpec(memory_space=pl.ANY))
    if len(extra) > 1:
        small = pl.BlockSpec(extra[1].shape, lambda s: (0, 0))
        specs += [small, small]
        out_specs.append(small)
        out_shape.append(jax.ShapeDtypeStruct(extra[1].shape, jnp.float32))
    return pl.pallas_call(
        lambda *refs: gram_kernel(1.0 / total_frames, *refs),
        grid=(steps,),
        in_specs=specs,
        out_specs=out_specs,
        out_shape=out_shape,
        scratch_shapes=[pltpu.VMEM((count * (tiles + 1), 128), jnp.float32)],
        input_output_aliases={3: 0} if extra else {},
        compiler_params=pltpu.CompilerParams(vmem_limit_bytes=VMEM),
        cost_estimate=pl.CostEstimate(
            flops=4 * steps * count * inputs * 256, bytes_accessed=steps << 20, transcendentals=0
        ),
        name="gram",
    )(*ops)


def on_device(voltages, pfb_window, channel_map, beam_layout):
    feed_count = lax.axis_size("feed")
    rep_count = lax.axis_size("rep")
    inp_dev, own_samples = voltages.shape
    total_frames = own_samples // DFT * rep_count
    inputs = inp_dev * feed_count
    slots = 2 * CHANNELS // feed_count
    swap = [(0, 1), (1, 0)]
    margin = lax.ppermute(voltages[:, own_samples - (TAPS - 1) * DFT :], "rep", [(0, 1)])
    outgoing = filtered(
        voltages, margin, pfb_window.reshape(1, -1), channel_map.reshape(1, -1), feed_count
    )
    own = lax.all_to_all(outgoing, "feed", split_axis=0, concat_axis=0, tiled=True)
    beam_own = beams(own, beam_layout.reshape(1, -1), 1.0 / (total_frames * CYL * POS))
    others, at = [], 0
    for part in PARTS:
        source = own if at + part < slots // 2 else lax.optimization_barrier((own, beam_own))[0]
        others.append(lax.ppermute(source[:, at * 128 : (at + part) * 128], "rep", swap))
        at += part
    beam_other = lax.ppermute(beam_own, "rep", swap)
    rep = lax.axis_index("rep").reshape(1)
    count = inputs // 2 // rep_count
    held, first = (), 0
    for part, other in zip(PARTS, others):
        if first + part == slots // 2:
            held += (beam_own, beam_other)
        held = tuple(gram(rep, own, other, first, held, count, total_frames))
        first += part
    summed, beam_power = held
    tiles = inputs // 128
    visibilities = summed.reshape(count, slots, tiles, 2, 128).transpose(0, 1, 3, 2, 4)
    return visibilities.reshape(count, slots, 2, inputs), beam_power


def solution(mesh):
    return jax.shard_map(
        on_device,
        mesh=mesh,
        in_specs=(P("feed", "rep"), P(), P(), P()),
        out_specs=(P("rep", "feed", None, None), P("feed", None)),
        check_vma=False,
    )
```

```python
import math

import jax
import jax.numpy as jnp
import numpy as np
from jax import lax
from jax.experimental import pallas as pl
from jax.experimental.pallas import tpu as pltpu
from jax.sharding import PartitionSpec as P

CYL = 4
POS = 128
DFT = 2048
CHANNELS = 512
CH0 = 256
TAPS = 4
HALF = DFT // 2
VMEM = 24 * 1024 * 1024
GROUPS = 4
HEAD = 4
PARTS = (2, 1, 1)
NT = (((1,), (1,)), ((), ()))


def wave_columns():
    samples = np.arange(HALF)
    tables = []
    for parity in range(2):
        bins = CH0 + np.arange(parity, CHANNELS, 2)
        angles = (samples[:, None] * bins[None, :] % DFT) * (2.0 * np.pi / DFT)
        tables.append(np.concatenate([np.cos(angles), -np.sin(angles)], axis=1))
    return np.stack(tables).astype(np.float32).astype(jnp.bfloat16)


def order_table(inputs, frames):
    frame, feed = np.meshgrid(np.arange(frames), np.arange(inputs), indexing="ij")
    target = (feed * frames + frame).reshape(-1)
    table = np.zeros((target.size, target.size), np.float32)
    table[target, np.arange(target.size)] = 1.0
    return table.astype(jnp.bfloat16)


def position_tables():
    places = np.arange(POS)
    angles = (places[:, None] * places[None, :] % POS) * (2.0 * np.pi / POS)
    tables = np.concatenate([np.cos(angles), np.sin(angles)])
    return tables.astype(np.float32).astype(jnp.bfloat16)


def tap_sums(window, volt_of, blocks, frames, first, last):
    inputs = blocks.shape[1] // frames

    def chunk(j, carry):
        low = pl.multiple_of(j * 128, 128)
        sums = []
        for at in (low, pl.multiple_of(low + HALF, 128)):
            weights = [
                jnp.broadcast_to(window[:, pl.ds(t * DFT + at, 128)], (inputs, 128))
                for t in range(TAPS)
            ]
            held = [volt_of(first + t + 1 - TAPS, at) for t in range(TAPS - 1)]
            column = []
            for f in range(first, last):
                held.append(volt_of(f, at))
                total = None
                for t in range(TAPS):
                    if held[t] is not None:
                        term = held[t] * weights[t]
                        total = term if total is None else total + term
                held = held[1:]
                column.append(total)
            sums.append(column)
        for f in range(0, last - first, 2):
            for parity in range(2):
                pair = []
                for k in (f, f + 1):
                    low_sum, high_sum = sums[0][k], sums[1][k]
                    pair.append(low_sum - high_sum if parity else low_sum + high_sum)
                at = (first + f) * inputs
                blocks[parity, at : at + 2 * inputs, pl.ds(low, 128)] = jnp.concatenate(
                    pair, axis=0
                ).astype(jnp.bfloat16)
        return carry

    lax.fori_loop(0, HALF // 128, chunk, 0)


def sums_kernel(
    chans, volt_hbm, window_hbm, slots_hbm, waves_hbm, order_hbm,
    blocks, pick, head, window, waves, order, volt, slots, sems,
):
    inputs = volt.shape[0]
    frames = volt.shape[1] // DFT
    dests = pick.shape[0] // chans
    group = frames // GROUPS
    span = group * DFT
    copies = [
        pltpu.make_async_copy(slots_hbm, slots, sems.at[GROUPS]),
        pltpu.make_async_copy(window_hbm, window, sems.at[GROUPS + 1]),
    ]
    for g in range(GROUPS):
        copies.append(
            pltpu.make_async_copy(
                volt_hbm.at[:, pl.ds(g * span, span)], volt.at[:, pl.ds(g * span, span)], sems.at[g]
            )
        )
    copies.append(pltpu.make_async_copy(waves_hbm, waves, sems.at[GROUPS + 2]))
    copies.append(pltpu.make_async_copy(order_hbm, order, sems.at[GROUPS + 3]))
    for copy in copies:
        copy.start()

    half_ch = CHANNELS // 2
    place = lax.broadcasted_iota(jnp.int32, (dests, CHANNELS), 1)
    channel = jnp.where(place < half_ch, 2 * place, 2 * (place - half_ch) + 1)
    dest = lax.broadcasted_iota(jnp.int32, (dests, CHANNELS), 0)
    copies[0].wait()
    held_by = slots[...].astype(jnp.float32)
    for c in range(chans):
        wanted = jnp.sum(
            jnp.where(place == dest * chans + c, held_by, 0.0), axis=1, keepdims=True
        ).astype(jnp.int32)
        pick[c * dests : (c + 1) * dests, :] = (
            (channel == wanted).astype(jnp.float32).astype(jnp.bfloat16)
        )
    copies[1].wait()
    window[...] = window[...] * (1.0 / math.sqrt(TAPS * CHANNELS))

    def volt_of(f, at):
        return None if f < 0 else volt[:, pl.ds(f * DFT + at, 128)].astype(jnp.float32)

    for g in range(GROUPS):
        copies[2 + g].wait()
        tap_sums(window, volt_of, blocks, frames, g * group, (g + 1) * group)
    head[...] = volt[:, : head.shape[1]]
    for copy in copies[2 + GROUPS :]:
        copy.wait()


def spectra_kernel(
    blocks, margin, head, window, pick, waves, order, out, first, spectra, sorted_, rows
):
    inputs = head.shape[0]
    columns = blocks.shape[1]
    frames = columns // inputs
    dests = out.shape[0] // inputs
    chans = pick.shape[0] // dests
    half_ch = CHANNELS // 2

    def volt_of(f, at):
        source, f = (margin, f + TAPS - 1) if f < 0 else (head, f)
        return source[:, pl.ds(f * DFT + at, 128)].astype(jnp.float32)

    tap_sums(window, volt_of, first, HEAD, 0, HEAD)
    for parity in range(2):
        sums = jnp.concatenate([first[parity], blocks[parity, HEAD * inputs :, :]], axis=0)
        spectra[:, parity * CHANNELS : (parity + 1) * CHANNELS] = jnp.dot(
            sums, waves[parity], preferred_element_type=jnp.float32
        ).astype(jnp.bfloat16)
    for parity in range(2):
        for part in range(2):
            at = parity * CHANNELS + part * half_ch
            turned = jnp.dot(
                order[...], spectra[:, at : at + half_ch], preferred_element_type=jnp.float32
            ).astype(jnp.bfloat16)
            for i in range(inputs):
                to = (2 * i + part) * frames
                sorted_[to : to + frames, parity * half_ch : (parity + 1) * half_ch] = turned[
                    i * frames : (i + 1) * frames, :
                ]
    wide = 2 * frames
    pitch = inputs + 1
    for pair in range(0, inputs, 2):
        picked = lax.dot_general(
            pick[...],
            sorted_[pair * wide : (pair + 2) * wide, :],
            NT,
            preferred_element_type=jnp.float32,
        )
        for c in range(chans):
            for i in range(2):
                rows[pl.ds(c * dests * pitch + pair + i, dests, stride=pitch), :] = picked[
                    c * dests : (c + 1) * dests, i * wide : (i + 1) * wide
                ]
    for c in range(chans):
        for dest in range(0, dests, 2):
            at = (c * dests + dest) * pitch
            pair = [rows[at + k * pitch : at + k * pitch + inputs, :] for k in range(2)]
            out[dest * inputs : (dest + 2) * inputs, c * wide : (c + 1) * wide] = jnp.concatenate(
                pair, axis=0
            ).astype(jnp.bfloat16)


def tap_blocks(volt, window, slots, dests):
    inputs, own = volt.shape
    chans = slots.shape[1] // dests
    vmem = pl.BlockSpec(memory_space=pltpu.VMEM)
    hbm = pl.BlockSpec(memory_space=pltpu.HBM)
    waves, order = jnp.asarray(wave_columns()), jnp.asarray(order_table(inputs, own // DFT))
    return pl.pallas_call(
        lambda *refs: sums_kernel(chans, *refs),
        in_specs=[hbm] * 5,
        out_specs=[vmem] * 6,
        out_shape=[
            jax.ShapeDtypeStruct((2, inputs * own // DFT, HALF), jnp.bfloat16),
            jax.ShapeDtypeStruct((chans * dests, CHANNELS), jnp.bfloat16),
            jax.ShapeDtypeStruct((inputs, HEAD * DFT), jnp.bfloat16),
            jax.ShapeDtypeStruct(window.shape, jnp.float32),
            jax.ShapeDtypeStruct(waves.shape, jnp.bfloat16),
            jax.ShapeDtypeStruct(order.shape, jnp.bfloat16),
        ],
        scratch_shapes=[
            pltpu.VMEM(volt.shape, jnp.bfloat16),
            pltpu.VMEM(slots.shape, jnp.int32),
            pltpu.SemaphoreType.DMA((GROUPS + 4,)),
        ],
        compiler_params=pltpu.CompilerParams(vmem_limit_bytes=VMEM),
        cost_estimate=pl.CostEstimate(
            flops=2 * inputs * own * TAPS, bytes_accessed=8 << 20, transcendentals=0
        ),
        name="tap_sums",
    )(*(pltpu.with_memory_space_constraint(x, pltpu.HBM) for x in (volt, window, slots, waves, order)))


def filtered(volt, margin, window, slots, dests):
    inputs, own = volt.shape
    frames = own // DFT
    chans = slots.shape[1] // dests
    columns = inputs * frames
    vmem = pl.BlockSpec(memory_space=pltpu.VMEM)
    blocks, pick, head, taps, waves, order = tap_blocks(volt, window, slots, dests)
    return pl.pallas_call(
        spectra_kernel,
        in_specs=[vmem] * 7,
        out_specs=vmem,
        out_shape=jax.ShapeDtypeStruct((dests * inputs, chans * 2 * frames), jnp.bfloat16),
        scratch_shapes=[
            pltpu.VMEM((2, HEAD * inputs, HALF), jnp.bfloat16),
            pltpu.VMEM((columns, 2 * CHANNELS), jnp.bfloat16),
            pltpu.VMEM((2 * columns, CHANNELS), jnp.bfloat16),
            pltpu.VMEM((chans * dests * (inputs + 1), 2 * frames), jnp.float32),
        ],
        compiler_params=pltpu.CompilerParams(vmem_limit_bytes=VMEM),
        cost_estimate=pl.CostEstimate(
            flops=2 * columns * CHANNELS * 4 * 1024, bytes_accessed=8 << 20, transcendentals=0
        ),
        name="spectra",
    )(blocks, margin, head, taps, pick, waves, order)


def beam_kernel(scale, own, layout, tables, out, mixer, mixed):
    inputs = own.shape[0]
    chans = own.shape[1] // 128
    half = CYL * POS
    lane = lax.broadcasted_iota(jnp.int32, (POS, 128), 1)
    first = lane < 64
    collected = jnp.zeros((POS, 128), jnp.float32)
    feed = lax.broadcasted_iota(jnp.int32, (inputs, POS), 0)
    for h in range(2):
        for y in range(CYL):
            at = h * half + y * POS
            hit = (feed == layout[:, at : at + POS]).astype(jnp.float32).astype(jnp.bfloat16)
            mixer[y * 2 * POS : (y + 1) * 2 * POS, :] = lax.dot_general(
                tables[...], hit, NT, preferred_element_type=jnp.float32
            ).astype(jnp.bfloat16)
        mixed[...] = jnp.dot(mixer[...], own[...], preferred_element_type=jnp.float32)

        def turned(value):
            other = pltpu.roll(value, 64, 1)
            return jnp.where(first, other, -other)

        for c in range(chans):
            at = c * 128
            north = []
            for y in range(CYL):
                base = y * 2 * POS
                cosine = mixed[base : base + POS, at : at + 128]
                sine = mixed[base + POS : base + 2 * POS, at : at + 128]
                north.append(cosine + turned(sine))
            even, odd = north[0] + north[2], north[1] + north[3]
            gap, step = north[0] - north[2], turned(north[1] - north[3])
            easts = [even + odd, gap + step, even - odd, gap - step]
            for e, east in enumerate(easts):
                power = jnp.sum(east * east, axis=1, keepdims=True)
                collected = jnp.where(lane == e * 2 * chans + c * 2 + h, power, collected)
    turned_over = collected.T
    for e in range(CYL):
        out[:, e * POS : (e + 1) * POS] = turned_over[e * 2 * chans : (e + 1) * 2 * chans, :] * scale


def beams(own, layout, scale):
    inputs, wide = own.shape
    chans = wide // 128
    return pl.pallas_call(
        lambda *refs: beam_kernel(scale, *refs),
        out_shape=jax.ShapeDtypeStruct((2 * chans, CYL * POS), jnp.float32),
        scratch_shapes=[
            pltpu.VMEM((CYL * 2 * POS, inputs), jnp.bfloat16),
            pltpu.VMEM((CYL * 2 * POS, wide), jnp.float32),
        ],
        compiler_params=pltpu.CompilerParams(vmem_limit_bytes=VMEM),
        cost_estimate=pl.CostEstimate(
            flops=4 * 1024 * inputs * wide, bytes_accessed=4 << 20, transcendentals=0
        ),
        name="beams",
    )(own, layout, position_tables())


def gram_kernel(scale, rep, own, other, *refs):
    out, rows = refs[-2:]
    if len(refs) > 3:
        beam_own, beam_other, out, beam, rows = refs[-5:]
        beam[...] = beam_own[...] + beam_other[...]
    step = pl.program_id(0)
    count, _, tiles, _ = out.shape
    inputs = own.shape[0]
    pitch = tiles + 1
    start = pl.multiple_of((step % 2) * (inputs // 2) + rep[0] * count, count)
    lane = lax.broadcasted_iota(jnp.int32, (count, 128), 1)
    plain, turned = [], []
    for source in (own, other):
        part = source[pl.ds(start, count), :]
        plain.append(part)
        swapped = pltpu.roll(part.astype(jnp.float32), 64, 1)
        turned.append(jnp.where(lane < 64, swapped, -swapped).astype(jnp.bfloat16))
    left = jnp.concatenate(
        [jnp.concatenate(plain, axis=1), jnp.concatenate(turned, axis=1)], axis=0
    )
    for at in range(0, inputs, 256):
        right = jnp.concatenate([own[at : at + 256, :], other[at : at + 256, :]], axis=1)
        products = lax.dot_general(left, right, NT, preferred_element_type=jnp.float32)
        for tile in range(2):
            for part in range(2):
                rows[pl.ds((at // 128 + tile) * 2 + part, count, stride=pitch), :] = products[
                    part * count : (part + 1) * count, tile * 128 : (tile + 1) * 128
                ]
    for r in range(count):
        out[r, 0] = (rows[r * pitch : r * pitch + tiles, :] * scale).astype(jnp.bfloat16)


def gram(rep, own, other, first, extra, count, total_frames):
    inputs, wide = own.shape
    slots = 2 * (wide // 128)
    steps = 2 * (other.shape[1] // 128)
    tiles = inputs // 64
    ops = [rep, own, other, *extra]
    specs = [
        pl.BlockSpec(memory_space=pltpu.SMEM),
        pl.BlockSpec((inputs, 128), lambda s: (0, first + s // 2)),
        pl.BlockSpec((inputs, 128), lambda s: (0, s // 2)),
    ]
    out_specs = [pl.BlockSpec((count, 1, tiles, 128), lambda s: (0, s + 2 * first, 0, 0))]
    out_shape = [jax.ShapeDtypeStruct((count, slots, tiles, 128), jnp.bfloat16)]
    if extra:
        specs.append(pl.BlockSpec(memory_space=pl.ANY))
    if len(extra) > 1:
        small = pl.BlockSpec(extra[1].shape, lambda s: (0, 0))
        specs += [small, small]
        out_specs.append(small)
        out_shape.append(jax.ShapeDtypeStruct(extra[1].shape, jnp.float32))
    return pl.pallas_call(
        lambda *refs: gram_kernel(1.0 / total_frames, *refs),
        grid=(steps,),
        in_specs=specs,
        out_specs=out_specs,
        out_shape=out_shape,
        scratch_shapes=[pltpu.VMEM((count * (tiles + 1), 128), jnp.float32)],
        input_output_aliases={3: 0} if extra else {},
        compiler_params=pltpu.CompilerParams(vmem_limit_bytes=VMEM),
        cost_estimate=pl.CostEstimate(
            flops=4 * steps * count * inputs * 256, bytes_accessed=steps << 20, transcendentals=0
        ),
        name="gram",
    )(*ops)


def on_device(voltages, pfb_window, channel_map, beam_layout):
    feed_count = lax.axis_size("feed")
    rep_count = lax.axis_size("rep")
    inp_dev, own_samples = voltages.shape
    total_frames = own_samples // DFT * rep_count
    inputs = inp_dev * feed_count
    slots = 2 * CHANNELS // feed_count
    swap = [(0, 1), (1, 0)]
    margin = lax.ppermute(voltages[:, own_samples - (TAPS - 1) * DFT :], "rep", [(0, 1)])
    outgoing = filtered(
        voltages, margin, pfb_window.reshape(1, -1), channel_map.reshape(1, -1), feed_count
    )
    own = lax.all_to_all(outgoing, "feed", split_axis=0, concat_axis=0, tiled=True)
    beam_own = beams(own, beam_layout.reshape(1, -1), 1.0 / (total_frames * CYL * POS))
    others, at = [], 0
    for part in PARTS:
        source = own if at + part < slots // 2 else lax.optimization_barrier((own, beam_own))[0]
        others.append(lax.ppermute(source[:, at * 128 : (at + part) * 128], "rep", swap))
        at += part
    beam_other = lax.ppermute(beam_own, "rep", swap)
    rep = lax.axis_index("rep").reshape(1)
    count = inputs // 2 // rep_count
    held, first = (), 0
    for part, other in zip(PARTS, others):
        if first + part == slots // 2:
            held += (beam_own, beam_other)
        held = tuple(gram(rep, own, other, first, held, count, total_frames))
        first += part
    summed, beam_power = held
    tiles = inputs // 128
    visibilities = summed.reshape(count, slots, tiles, 2, 128).transpose(0, 1, 3, 2, 4)
    return visibilities.reshape(count, slots, 2, inputs), beam_power


def solution(mesh):
    return jax.shard_map(
        on_device,
        mesh=mesh,
        in_specs=(P("feed", "rep"), P(), P(), P()),
        out_specs=(P("rep", "feed", None, None), P("feed", None)),
        check_vma=False,
    )
```

```python
import math

import jax
import jax.numpy as jnp
import numpy as np
from jax import lax
from jax.experimental import pallas as pl
from jax.experimental.pallas import tpu as pltpu
from jax.sharding import PartitionSpec as P

CYL = 4
POS = 128
DFT = 2048
CHANNELS = 512
CH0 = 256
TAPS = 4
HALF = DFT // 2
VMEM = 24 * 1024 * 1024
GROUPS = 4
PIECE = 64
HEAD = 4
PARTS = (2, 1, 1)
NT = (((1,), (1,)), ((), ()))


def wave_columns():
    samples = np.arange(HALF)
    tables = []
    for parity in range(2):
        bins = CH0 + np.arange(parity, CHANNELS, 2)
        angles = (samples[:, None] * bins[None, :] % DFT) * (2.0 * np.pi / DFT)
        tables.append(np.concatenate([np.cos(angles), -np.sin(angles)], axis=1))
    return np.stack(tables).astype(np.float32).astype(jnp.bfloat16)


def position_tables():
    places = np.arange(POS)
    angles = (places[:, None] * places[None, :] % POS) * (2.0 * np.pi / POS)
    tables = np.concatenate([np.cos(angles), np.sin(angles)])
    return tables.astype(np.float32).astype(jnp.bfloat16)


def tap_sums(window, volt_of, blocks, frames, first, last):
    inputs = blocks.shape[1] // frames

    def chunk(j, carry):
        low = pl.multiple_of(j * 128, 128)
        sums = []
        for at in (low, pl.multiple_of(low + HALF, 128)):
            weights = [
                jnp.broadcast_to(window[:, pl.ds(t * DFT + at, 128)], (inputs, 128))
                for t in range(TAPS)
            ]
            held = [volt_of(first + t + 1 - TAPS, at) for t in range(TAPS - 1)]
            column = []
            for f in range(first, last):
                held.append(volt_of(f, at))
                total = None
                for t in range(TAPS):
                    if held[t] is not None:
                        term = held[t] * weights[t]
                        total = term if total is None else total + term
                held = held[1:]
                column.append(total)
            sums.append(column)
        for f in range(0, last - first, 2):
            for parity in range(2):
                pair = []
                for k in (f, f + 1):
                    low_sum, high_sum = sums[0][k], sums[1][k]
                    pair.append(low_sum - high_sum if parity else low_sum + high_sum)
                at = (first + f) * inputs
                blocks[parity, at : at + 2 * inputs, pl.ds(low, 128)] = jnp.concatenate(
                    pair, axis=0
                ).astype(jnp.bfloat16)
        return carry

    lax.fori_loop(0, HALF // 128, chunk, 0)


def sums_kernel(
    chans, volt_hbm, window_hbm, slots_hbm, waves_hbm,
    blocks, pick, head, window, waves, order, volt, slots, sems,
):
    inputs = volt.shape[0]
    frames = volt.shape[1] // DFT
    dests = pick.shape[0] // chans
    group = frames // GROUPS
    span = group * DFT
    copies = [
        pltpu.make_async_copy(slots_hbm, slots, sems.at[GROUPS]),
        pltpu.make_async_copy(window_hbm, window, sems.at[GROUPS + 1]),
    ]
    for g in range(GROUPS):
        copies.append(
            pltpu.make_async_copy(
                volt_hbm.at[:, pl.ds(g * span, span)], volt.at[:, pl.ds(g * span, span)], sems.at[g]
            )
        )
    copies.append(pltpu.make_async_copy(waves_hbm, waves, sems.at[GROUPS + 2]))
    for copy in copies:
        copy.start()

    half_ch = CHANNELS // 2
    place = lax.broadcasted_iota(jnp.int32, (dests, CHANNELS), 1)
    channel = jnp.where(place < half_ch, 2 * place, 2 * (place - half_ch) + 1)
    dest = lax.broadcasted_iota(jnp.int32, (dests, CHANNELS), 0)
    copies[0].wait()
    held_by = slots[...].astype(jnp.float32)
    for c in range(chans):
        wanted = jnp.sum(
            jnp.where(place == dest * chans + c, held_by, 0.0), axis=1, keepdims=True
        ).astype(jnp.int32)
        pick[c * dests : (c + 1) * dests, :] = (
            (channel == wanted).astype(jnp.float32).astype(jnp.bfloat16)
        )
    row = lax.broadcasted_iota(jnp.int32, order.shape, 0)
    column = lax.broadcasted_iota(jnp.int32, order.shape, 1)
    source = (row % frames) * inputs + row // frames
    order[...] = (column == source).astype(jnp.float32).astype(jnp.bfloat16)
    copies[1].wait()
    window[...] = window[...] * (1.0 / math.sqrt(TAPS * CHANNELS))

    def volt_of(f, at):
        return None if f < 0 else volt[:, pl.ds(f * DFT + at, 128)].astype(jnp.float32)

    for g in range(GROUPS):
        copies[2 + g].wait()
        tap_sums(window, volt_of, blocks, frames, g * group, (g + 1) * group)
    head[...] = volt[:, : head.shape[1]]
    for copy in copies[2 + GROUPS :]:
        copy.wait()


def spectra_kernel(
    blocks, margin, head, window, pick, waves, order, out, first, spectra, sorted_, rows
):
    inputs = head.shape[0]
    columns = blocks.shape[1]
    frames = columns // inputs
    dests = out.shape[0] // inputs
    chans = pick.shape[0] // dests
    half_ch = CHANNELS // 2

    def volt_of(f, at):
        source, f = (margin, f + TAPS - 1) if f < 0 else (head, f)
        return source[:, pl.ds(f * DFT + at, 128)].astype(jnp.float32)

    tap_sums(window, volt_of, first, HEAD, 0, HEAD)
    for parity in range(2):
        sums = jnp.concatenate([first[parity], blocks[parity, HEAD * inputs :, :]], axis=0)
        spectra[:, parity * CHANNELS : (parity + 1) * CHANNELS] = jnp.dot(
            sums, waves[parity], preferred_element_type=jnp.float32
        ).astype(jnp.bfloat16)
    for parity in range(2):
        for part in range(2):
            at = parity * CHANNELS + part * half_ch
            turned = jnp.dot(
                order[...], spectra[:, at : at + half_ch], preferred_element_type=jnp.float32
            ).astype(jnp.bfloat16)
            for i in range(inputs):
                to = (2 * i + part) * frames
                sorted_[to : to + frames, parity * half_ch : (parity + 1) * half_ch] = turned[
                    i * frames : (i + 1) * frames, :
                ]
    wide = 2 * frames
    pitch = inputs + 1
    for pair in range(0, inputs, 2):
        picked = lax.dot_general(
            pick[...],
            sorted_[pair * wide : (pair + 2) * wide, :],
            NT,
            preferred_element_type=jnp.float32,
        )
        for c in range(chans):
            for i in range(2):
                rows[pl.ds(c * dests * pitch + pair + i, dests, stride=pitch), :] = picked[
                    c * dests : (c + 1) * dests, i * wide : (i + 1) * wide
                ]
    for c in range(chans):
        for dest in range(0, dests, 2):
            at = (c * dests + dest) * pitch
            pair = [rows[at + k * pitch : at + k * pitch + inputs, :] for k in range(2)]
            out[dest * inputs : (dest + 2) * inputs, c * wide : (c + 1) * wide] = jnp.concatenate(
                pair, axis=0
            ).astype(jnp.bfloat16)


def tap_blocks(volt, window, slots, dests):
    inputs, own = volt.shape
    chans = slots.shape[1] // dests
    vmem = pl.BlockSpec(memory_space=pltpu.VMEM)
    hbm = pl.BlockSpec(memory_space=pltpu.HBM)
    waves = jnp.asarray(wave_columns())
    return pl.pallas_call(
        lambda *refs: sums_kernel(chans, *refs),
        in_specs=[hbm] * 4,
        out_specs=[vmem] * 6,
        out_shape=[
            jax.ShapeDtypeStruct((2, inputs * own // DFT, HALF), jnp.bfloat16),
            jax.ShapeDtypeStruct((chans * dests, CHANNELS), jnp.bfloat16),
            jax.ShapeDtypeStruct((inputs, HEAD * DFT), jnp.bfloat16),
            jax.ShapeDtypeStruct(window.shape, jnp.float32),
            jax.ShapeDtypeStruct(waves.shape, jnp.bfloat16),
            jax.ShapeDtypeStruct((inputs * own // DFT,) * 2, jnp.bfloat16),
        ],
        scratch_shapes=[
            pltpu.VMEM(volt.shape, jnp.bfloat16),
            pltpu.VMEM(slots.shape, jnp.int32),
            pltpu.SemaphoreType.DMA((GROUPS + 3,)),
        ],
        compiler_params=pltpu.CompilerParams(vmem_limit_bytes=VMEM),
        cost_estimate=pl.CostEstimate(
            flops=2 * inputs * own * TAPS, bytes_accessed=8 << 20, transcendentals=0
        ),
        name="tap_sums",
    )(*(pltpu.with_memory_space_constraint(x, pltpu.HBM) for x in (volt, window, slots, waves)))


def filtered(volt, margin, window, slots, dests):
    inputs, own = volt.shape
    frames = own // DFT
    chans = slots.shape[1] // dests
    columns = inputs * frames
    vmem = pl.BlockSpec(memory_space=pltpu.VMEM)
    blocks, pick, head, taps, waves, order = tap_blocks(volt, window, slots, dests)
    return pl.pallas_call(
        spectra_kernel,
        in_specs=[vmem] * 7,
        out_specs=vmem,
        out_shape=jax.ShapeDtypeStruct((dests * inputs, chans * 2 * frames), jnp.bfloat16),
        scratch_shapes=[
            pltpu.VMEM((2, HEAD * inputs, HALF), jnp.bfloat16),
            pltpu.VMEM((columns, 2 * CHANNELS), jnp.bfloat16),
            pltpu.VMEM((2 * columns, CHANNELS), jnp.bfloat16),
            pltpu.VMEM(((chans * dests + 8) * (inputs + 1), 2 * frames), jnp.float32),
        ],
        compiler_params=pltpu.CompilerParams(vmem_limit_bytes=VMEM),
        cost_estimate=pl.CostEstimate(
            flops=2 * columns * CHANNELS * 4 * 1024, bytes_accessed=8 << 20, transcendentals=0
        ),
        name="spectra",
    )(blocks, margin, head, taps, pick, waves, order)


def beam_kernel(scale, own, layout, tables, out, mixer, mixed):
    inputs = own.shape[0]
    chans = own.shape[1] // 128
    half = CYL * POS
    lane = lax.broadcasted_iota(jnp.int32, (POS, 128), 1)
    first = lane < 64
    collected = jnp.zeros((POS, 128), jnp.float32)
    feed = lax.broadcasted_iota(jnp.int32, (inputs, POS), 0)
    for h in range(2):
        for y in range(CYL):
            at = h * half + y * POS
            hit = (feed == layout[:, at : at + POS]).astype(jnp.float32).astype(jnp.bfloat16)
            mixer[y * 2 * POS : (y + 1) * 2 * POS, :] = lax.dot_general(
                tables[...], hit, NT, preferred_element_type=jnp.float32
            ).astype(jnp.bfloat16)
        mixed[...] = jnp.dot(mixer[...], own[...], preferred_element_type=jnp.float32)

        def turned(value):
            other = pltpu.roll(value, 64, 1)
            return jnp.where(first, other, -other)

        for c in range(chans):
            at = c * 128
            north = []
            for y in range(CYL):
                base = y * 2 * POS
                cosine = mixed[base : base + POS, at : at + 128]
                sine = mixed[base + POS : base + 2 * POS, at : at + 128]
                north.append(cosine + turned(sine))
            even, odd = north[0] + north[2], north[1] + north[3]
            gap, step = north[0] - north[2], turned(north[1] - north[3])
            easts = [even + odd, gap + step, even - odd, gap - step]
            for e, east in enumerate(easts):
                power = jnp.sum(east * east, axis=1, keepdims=True)
                collected = jnp.where(lane == e * 2 * chans + c * 2 + h, power, collected)
    turned_over = collected.T
    for e in range(CYL):
        out[:, e * POS : (e + 1) * POS] = turned_over[e * 2 * chans : (e + 1) * 2 * chans, :] * scale


def beams(own, layout, scale):
    inputs, wide = own.shape
    chans = wide // 128
    return pl.pallas_call(
        lambda *refs: beam_kernel(scale, *refs),
        out_shape=jax.ShapeDtypeStruct((2 * chans, CYL * POS), jnp.float32),
        scratch_shapes=[
            pltpu.VMEM((CYL * 2 * POS, inputs), jnp.bfloat16),
            pltpu.VMEM((CYL * 2 * POS, wide), jnp.float32),
        ],
        compiler_params=pltpu.CompilerParams(vmem_limit_bytes=VMEM),
        cost_estimate=pl.CostEstimate(
            flops=4 * 1024 * inputs * wide, bytes_accessed=4 << 20, transcendentals=0
        ),
        name="beams",
    )(own, layout, position_tables())


def gram_kernel(scale, first, rep, own, other, *refs):
    out, rows, stage, sems = refs[-4:]
    copies = []
    if len(refs) > 5:
        beam_own, beam_other, out, beam_out, beam, rows, stage, sems = refs[-8:]
        beam[...] = beam_own[...] + beam_other[...]
        copies.append(pltpu.make_async_copy(beam, beam_out, sems.at[0]))
        copies[0].start()
    count, _, tiles, _ = out.shape
    inputs = own.shape[0]
    pitch = tiles + 1
    lane = lax.broadcasted_iota(jnp.int32, (count, 128), 1)
    for c in range(other.shape[1] // 128):
        mine = pl.ds((first + c) * 128, 128)
        theirs = pl.ds(c * 128, 128)
        left = []
        for half in range(2):
            start = pl.multiple_of(half * (inputs // 2) + rep[0] * count, count)
            plain, turned = [], []
            for part in (own[pl.ds(start, count), mine], other[pl.ds(start, count), theirs]):
                plain.append(part)
                swapped = pltpu.roll(part.astype(jnp.float32), 64, 1)
                turned.append(jnp.where(lane < 64, swapped, -swapped).astype(jnp.bfloat16))
            left += [jnp.concatenate(plain, axis=1), jnp.concatenate(turned, axis=1)]
        left = jnp.concatenate(left, axis=0)
        for at in range(0, inputs, 256):
            right = jnp.concatenate([own[at : at + 256, mine], other[at : at + 256, theirs]], axis=1)
            products = lax.dot_general(left, right, NT, preferred_element_type=jnp.float32)
            for half in range(2):
                for part in range(2):
                    for tile in range(2):
                        to = half * count * pitch + (at // 128 + tile) * 2 + part
                        row = (2 * half + part) * count
                        rows[pl.ds(to, count, stride=pitch), :] = products[
                            row : row + count, tile * 128 : (tile + 1) * 128
                        ]
        for half in range(2):
            slot = 2 * c + half
            for piece in range(0, count, PIECE):
                for r in range(piece, piece + PIECE):
                    at = (half * count + r) * pitch
                    stage[slot, r] = (rows[at : at + tiles, :] * scale).astype(jnp.bfloat16)
                copies.append(
                    pltpu.make_async_copy(
                        stage.at[slot, pl.ds(piece, PIECE)],
                        out.at[pl.ds(piece, PIECE), 2 * first + slot],
                        sems.at[len(copies)],
                    )
                )
                copies[-1].start()
    for copy in copies:
        copy.wait()


def gram(rep, own, other, first, extra, count, total_frames):
    inputs, wide = own.shape
    slots = 2 * (wide // 128)
    steps = 2 * (other.shape[1] // 128)
    tiles = inputs // 64
    vmem = pl.BlockSpec(memory_space=pltpu.VMEM)
    hbm = pl.BlockSpec(memory_space=pltpu.HBM)
    specs = [pl.BlockSpec(memory_space=pltpu.SMEM), vmem, vmem]
    out_specs = [hbm]
    out_shape = [jax.ShapeDtypeStruct((count, slots, tiles, 128), jnp.bfloat16)]
    scratch = []
    if extra:
        specs.append(hbm)
    if len(extra) > 1:
        specs += [vmem, vmem]
        out_specs.append(hbm)
        out_shape.append(jax.ShapeDtypeStruct(extra[1].shape, jnp.float32))
        scratch.append(pltpu.VMEM(extra[1].shape, jnp.float32))
    return pl.pallas_call(
        lambda *refs: gram_kernel(1.0 / total_frames, first, *refs),
        in_specs=specs,
        out_specs=out_specs,
        out_shape=out_shape,
        scratch_shapes=scratch
        + [
            pltpu.VMEM(((2 * count + 8) * (tiles + 1), 128), jnp.float32),
            pltpu.VMEM((steps, count, tiles, 128), jnp.bfloat16),
            pltpu.SemaphoreType.DMA((1 + steps * (count // PIECE),)),
        ],
        input_output_aliases={3: 0} if extra else {},
        compiler_params=pltpu.CompilerParams(vmem_limit_bytes=VMEM),
        cost_estimate=pl.CostEstimate(
            flops=4 * steps * count * inputs * 256, bytes_accessed=steps << 20, transcendentals=0
        ),
        name="gram",
    )(rep, own, other, *extra)


def on_device(voltages, pfb_window, channel_map, beam_layout):
    feed_count = lax.axis_size("feed")
    rep_count = lax.axis_size("rep")
    inp_dev, own_samples = voltages.shape
    total_frames = own_samples // DFT * rep_count
    inputs = inp_dev * feed_count
    slots = 2 * CHANNELS // feed_count
    swap = [(0, 1), (1, 0)]
    margin = lax.ppermute(voltages[:, own_samples - (TAPS - 1) * DFT :], "rep", [(0, 1)])
    outgoing = filtered(
        voltages, margin, pfb_window.reshape(1, -1), channel_map.reshape(1, -1), feed_count
    )
    own = lax.all_to_all(outgoing, "feed", split_axis=0, concat_axis=0, tiled=True)
    beam_own = beams(own, beam_layout.reshape(1, -1), 1.0 / (total_frames * CYL * POS))
    others, at = [], 0
    for part in PARTS:
        source = own if at + part < slots // 2 else lax.optimization_barrier((own, beam_own))[0]
        others.append(lax.ppermute(source[:, at * 128 : (at + part) * 128], "rep", swap))
        at += part
    beam_other = lax.ppermute(beam_own, "rep", swap)
    rep = lax.axis_index("rep").reshape(1)
    count = inputs // 2 // rep_count
    held, first = (), 0
    for part, other in zip(PARTS, others):
        if first + part == slots // 2:
            held += (beam_own, beam_other)
        held = tuple(gram(rep, own, other, first, held, count, total_frames))
        first += part
    summed, beam_power = held
    tiles = inputs // 128
    visibilities = summed.reshape(count, slots, tiles, 2, 128).transpose(0, 1, 3, 2, 4)
    return visibilities.reshape(count, slots, 2, inputs), beam_power


def solution(mesh):
    return jax.shard_map(
        on_device,
        mesh=mesh,
        in_specs=(P("feed", "rep"), P(), P(), P()),
        out_specs=(P("rep", "feed", None, None), P("feed", None)),
        check_vma=False,
    )
```

```python
import math

import jax
import jax.numpy as jnp
import numpy as np
from jax import lax
from jax.experimental import pallas as pl
from jax.experimental.pallas import tpu as pltpu
from jax.sharding import PartitionSpec as P

CYL = 4
POS = 128
DFT = 2048
CHANNELS = 512
CH0 = 256
TAPS = 4
HALF = DFT // 2
VMEM = 24 * 1024 * 1024
GROUPS = 4
PIECE = 64
HEAD = 4
PARTS = (2, 1, 1)
NT = (((1,), (1,)), ((), ()))


def wave_columns():
    samples = np.arange(HALF)
    tables = []
    for parity in range(2):
        bins = CH0 + np.arange(parity, CHANNELS, 2)
        angles = (samples[:, None] * bins[None, :] % DFT) * (2.0 * np.pi / DFT)
        tables.append(np.concatenate([np.cos(angles), -np.sin(angles)], axis=1))
    return np.stack(tables).astype(np.float32).astype(jnp.bfloat16)


def position_tables():
    places = np.arange(POS)
    angles = (places[:, None] * places[None, :] % POS) * (2.0 * np.pi / POS)
    tables = np.concatenate([np.cos(angles), np.sin(angles)])
    return tables.astype(np.float32).astype(jnp.bfloat16)


def tap_sums(window, volt_of, blocks, frames, first, last):
    inputs = blocks.shape[1] // frames

    def chunk(j, carry):
        low = pl.multiple_of(j * 128, 128)
        sums = []
        for at in (low, pl.multiple_of(low + HALF, 128)):
            weights = [
                jnp.broadcast_to(window[:, pl.ds(t * DFT + at, 128)], (inputs, 128))
                for t in range(TAPS)
            ]
            held = [volt_of(first + t + 1 - TAPS, at) for t in range(TAPS - 1)]
            column = []
            for f in range(first, last):
                held.append(volt_of(f, at))
                total = None
                for t in range(TAPS):
                    if held[t] is not None:
                        term = held[t] * weights[t]
                        total = term if total is None else total + term
                held = held[1:]
                column.append(total)
            sums.append(column)
        for f in range(0, last - first, 2):
            for parity in range(2):
                pair = []
                for k in (f, f + 1):
                    low_sum, high_sum = sums[0][k], sums[1][k]
                    pair.append(low_sum - high_sum if parity else low_sum + high_sum)
                at = (first + f) * inputs
                blocks[parity, at : at + 2 * inputs, pl.ds(low, 128)] = jnp.concatenate(
                    pair, axis=0
                ).astype(jnp.bfloat16)
        return carry

    lax.fori_loop(0, HALF // 128, chunk, 0)


def sums_kernel(
    chans, volt_hbm, window_hbm, slots_hbm, waves_hbm,
    blocks, pick, head, window, waves, order, volt, slots, sems,
):
    inputs = volt.shape[0]
    frames = volt.shape[1] // DFT
    dests = pick.shape[0] // chans
    group = frames // GROUPS
    span = group * DFT
    copies = [
        pltpu.make_async_copy(slots_hbm, slots, sems.at[GROUPS]),
        pltpu.make_async_copy(window_hbm, window, sems.at[GROUPS + 1]),
    ]
    for g in range(GROUPS):
        copies.append(
            pltpu.make_async_copy(
                volt_hbm.at[:, pl.ds(g * span, span)], volt.at[:, pl.ds(g * span, span)], sems.at[g]
            )
        )
    copies.append(pltpu.make_async_copy(waves_hbm, waves, sems.at[GROUPS + 2]))
    for copy in copies:
        copy.start()

    half_ch = CHANNELS // 2
    place = lax.broadcasted_iota(jnp.int32, (dests, CHANNELS), 1)
    channel = jnp.where(place < half_ch, 2 * place, 2 * (place - half_ch) + 1)
    dest = lax.broadcasted_iota(jnp.int32, (dests, CHANNELS), 0)
    copies[0].wait()
    held_by = slots[...].astype(jnp.float32)
    for c in range(chans):
        wanted = jnp.sum(
            jnp.where(place == dest * chans + c, held_by, 0.0), axis=1, keepdims=True
        ).astype(jnp.int32)
        pick[c * dests : (c + 1) * dests, :] = (
            (channel == wanted).astype(jnp.float32).astype(jnp.bfloat16)
        )
    row = lax.broadcasted_iota(jnp.int32, order.shape, 0)
    column = lax.broadcasted_iota(jnp.int32, order.shape, 1)
    source = (row % frames) * inputs + row // frames
    order[...] = (column == source).astype(jnp.float32).astype(jnp.bfloat16)
    copies[1].wait()
    window[...] = window[...] * (1.0 / math.sqrt(TAPS * CHANNELS))

    def volt_of(f, at):
        return None if f < 0 else volt[:, pl.ds(f * DFT + at, 128)].astype(jnp.float32)

    for g in range(GROUPS):
        copies[2 + g].wait()
        tap_sums(window, volt_of, blocks, frames, g * group, (g + 1) * group)
    head[...] = volt[:, : head.shape[1]]
    for copy in copies[2 + GROUPS :]:
        copy.wait()


def spectra_kernel(
    blocks, margin, head, window, pick, waves, order, out, first, spectra, sorted_, rows
):
    inputs = head.shape[0]
    columns = blocks.shape[1]
    frames = columns // inputs
    dests = out.shape[0] // inputs
    chans = pick.shape[0] // dests
    half_ch = CHANNELS // 2

    def volt_of(f, at):
        source, f = (margin, f + TAPS - 1) if f < 0 else (head, f)
        return source[:, pl.ds(f * DFT + at, 128)].astype(jnp.float32)

    tap_sums(window, volt_of, first, HEAD, 0, HEAD)
    for parity in range(2):
        sums = jnp.concatenate([first[parity], blocks[parity, HEAD * inputs :, :]], axis=0)
        spectra[:, parity * CHANNELS : (parity + 1) * CHANNELS] = jnp.dot(
            sums, waves[parity], preferred_element_type=jnp.float32
        ).astype(jnp.bfloat16)
    for parity in range(2):
        for part in range(2):
            at = parity * CHANNELS + part * half_ch
            turned = jnp.dot(
                order[...], spectra[:, at : at + half_ch], preferred_element_type=jnp.float32
            ).astype(jnp.bfloat16)
            for i in range(inputs):
                to = (2 * i + part) * frames
                sorted_[to : to + frames, parity * half_ch : (parity + 1) * half_ch] = turned[
                    i * frames : (i + 1) * frames, :
                ]
    wide = 2 * frames
    pitch = inputs + 1
    for pair in range(0, inputs, 2):
        picked = lax.dot_general(
            pick[...],
            sorted_[pair * wide : (pair + 2) * wide, :],
            NT,
            preferred_element_type=jnp.float32,
        )
        for c in range(chans):
            for i in range(2):
                rows[pl.ds(c * dests * pitch + pair + i, dests, stride=pitch), :] = picked[
                    c * dests : (c + 1) * dests, i * wide : (i + 1) * wide
                ]
    for c in range(chans):
        for dest in range(0, dests, 2):
            at = (c * dests + dest) * pitch
            pair = [rows[at + k * pitch : at + k * pitch + inputs, :] for k in range(2)]
            out[dest * inputs : (dest + 2) * inputs, c * wide : (c + 1) * wide] = jnp.concatenate(
                pair, axis=0
            ).astype(jnp.bfloat16)


def tap_blocks(volt, window, slots, dests):
    inputs, own = volt.shape
    chans = slots.shape[1] // dests
    vmem = pl.BlockSpec(memory_space=pltpu.VMEM)
    hbm = pl.BlockSpec(memory_space=pltpu.HBM)
    waves = jnp.asarray(wave_columns())
    return pl.pallas_call(
        lambda *refs: sums_kernel(chans, *refs),
        in_specs=[hbm] * 4,
        out_specs=[vmem] * 6,
        out_shape=[
            jax.ShapeDtypeStruct((2, inputs * own // DFT, HALF), jnp.bfloat16),
            jax.ShapeDtypeStruct((chans * dests, CHANNELS), jnp.bfloat16),
            jax.ShapeDtypeStruct((inputs, HEAD * DFT), jnp.bfloat16),
            jax.ShapeDtypeStruct(window.shape, jnp.float32),
            jax.ShapeDtypeStruct(waves.shape, jnp.bfloat16),
            jax.ShapeDtypeStruct((inputs * own // DFT,) * 2, jnp.bfloat16),
        ],
        scratch_shapes=[
            pltpu.VMEM(volt.shape, jnp.bfloat16),
            pltpu.VMEM(slots.shape, jnp.int32),
            pltpu.SemaphoreType.DMA((GROUPS + 3,)),
        ],
        compiler_params=pltpu.CompilerParams(vmem_limit_bytes=VMEM),
        cost_estimate=pl.CostEstimate(
            flops=2 * inputs * own * TAPS, bytes_accessed=8 << 20, transcendentals=0
        ),
        name="tap_sums",
    )(*(pltpu.with_memory_space_constraint(x, pltpu.HBM) for x in (volt, window, slots, waves)))


def filtered(volt, margin, window, slots, dests):
    inputs, own = volt.shape
    frames = own // DFT
    chans = slots.shape[1] // dests
    columns = inputs * frames
    vmem = pl.BlockSpec(memory_space=pltpu.VMEM)
    blocks, pick, head, taps, waves, order = tap_blocks(volt, window, slots, dests)
    return pl.pallas_call(
        spectra_kernel,
        in_specs=[vmem] * 7,
        out_specs=vmem,
        out_shape=jax.ShapeDtypeStruct((dests * inputs, chans * 2 * frames), jnp.bfloat16),
        scratch_shapes=[
            pltpu.VMEM((2, HEAD * inputs, HALF), jnp.bfloat16),
            pltpu.VMEM((columns, 2 * CHANNELS), jnp.bfloat16),
            pltpu.VMEM((2 * columns, CHANNELS), jnp.bfloat16),
            pltpu.VMEM(((chans * dests + 8) * (inputs + 1), 2 * frames), jnp.float32),
        ],
        compiler_params=pltpu.CompilerParams(vmem_limit_bytes=VMEM),
        cost_estimate=pl.CostEstimate(
            flops=2 * columns * CHANNELS * 4 * 1024, bytes_accessed=8 << 20, transcendentals=0
        ),
        name="spectra",
    )(blocks, margin, head, taps, pick, waves, order)


def beam_kernel(scale, own, layout, tables, out, mixer, mixed):
    inputs = own.shape[0]
    chans = own.shape[1] // 128
    half = CYL * POS
    lane = lax.broadcasted_iota(jnp.int32, (POS, 128), 1)
    first = lane < 64
    collected = jnp.zeros((POS, 128), jnp.float32)
    feed = lax.broadcasted_iota(jnp.int32, (inputs, POS), 0)
    for h in range(2):
        for y in range(CYL):
            at = h * half + y * POS
            hit = (feed == layout[:, at : at + POS]).astype(jnp.float32).astype(jnp.bfloat16)
            mixer[y * 2 * POS : (y + 1) * 2 * POS, :] = lax.dot_general(
                tables[...], hit, NT, preferred_element_type=jnp.float32
            ).astype(jnp.bfloat16)
        mixed[...] = jnp.dot(mixer[...], own[...], preferred_element_type=jnp.float32)

        def turned(value):
            other = pltpu.roll(value, 64, 1)
            return jnp.where(first, other, -other)

        for c in range(chans):
            at = c * 128
            north = []
            for y in range(CYL):
                base = y * 2 * POS
                cosine = mixed[base : base + POS, at : at + 128]
                sine = mixed[base + POS : base + 2 * POS, at : at + 128]
                north.append(cosine + turned(sine))
            even, odd = north[0] + north[2], north[1] + north[3]
            gap, step = north[0] - north[2], turned(north[1] - north[3])
            easts = [even + odd, gap + step, even - odd, gap - step]
            for e, east in enumerate(easts):
                power = jnp.sum(east * east, axis=1, keepdims=True)
                collected = jnp.where(lane == e * 2 * chans + c * 2 + h, power, collected)
    turned_over = collected.T
    for e in range(CYL):
        out[:, e * POS : (e + 1) * POS] = turned_over[e * 2 * chans : (e + 1) * 2 * chans, :] * scale


def beams(own, layout, scale):
    inputs, wide = own.shape
    chans = wide // 128
    return pl.pallas_call(
        lambda *refs: beam_kernel(scale, *refs),
        out_shape=jax.ShapeDtypeStruct((2 * chans, CYL * POS), jnp.float32),
        scratch_shapes=[
            pltpu.VMEM((CYL * 2 * POS, inputs), jnp.bfloat16),
            pltpu.VMEM((CYL * 2 * POS, wide), jnp.float32),
        ],
        compiler_params=pltpu.CompilerParams(vmem_limit_bytes=VMEM),
        cost_estimate=pl.CostEstimate(
            flops=4 * 1024 * inputs * wide, bytes_accessed=4 << 20, transcendentals=0
        ),
        name="beams",
    )(own, layout, position_tables())


def gram_kernel(scale, first, rep, own, other, *refs):
    out, rows, stage, sems = refs[-4:]
    copies = []
    if len(refs) > 5:
        beam_own, beam_other, out, beam_out, beam, rows, stage, sems = refs[-8:]
        beam[...] = beam_own[...] + beam_other[...]
        copies.append(pltpu.make_async_copy(beam, beam_out, sems.at[0]))
        copies[0].start()
    count, _, tiles, _ = out.shape
    inputs = own.shape[0]
    pitch = tiles + 1
    lane = lax.broadcasted_iota(jnp.int32, (count, 128), 1)
    for c in range(other.shape[1] // 128):
        mine = pl.ds((first + c) * 128, 128)
        theirs = pl.ds(c * 128, 128)
        for half in range(2):
            start = pl.multiple_of(half * (inputs // 2) + rep[0] * count, count)
            plain, turned = [], []
            for part in (own[pl.ds(start, count), mine], other[pl.ds(start, count), theirs]):
                plain.append(part)
                swapped = pltpu.roll(part.astype(jnp.float32), 64, 1)
                turned.append(jnp.where(lane < 64, swapped, -swapped).astype(jnp.bfloat16))
            left = jnp.concatenate(
                [jnp.concatenate(plain, axis=1), jnp.concatenate(turned, axis=1)], axis=0
            )
            base = half * count * pitch
            for at in range(0, inputs, 256):
                right = jnp.concatenate(
                    [own[at : at + 256, mine], other[at : at + 256, theirs]], axis=1
                )
                products = lax.dot_general(left, right, NT, preferred_element_type=jnp.float32)
                for part in range(2):
                    for tile in range(2):
                        to = base + (at // 128 + tile) * 2 + part
                        rows[pl.ds(to, count, stride=pitch), :] = products[
                            part * count : (part + 1) * count, tile * 128 : (tile + 1) * 128
                        ]
            slot = 2 * c + half
            for piece in range(0, count, PIECE):
                for r in range(piece, piece + PIECE):
                    at = base + r * pitch
                    stage[slot, r] = (rows[at : at + tiles, :] * scale).astype(jnp.bfloat16)
                copies.append(
                    pltpu.make_async_copy(
                        stage.at[slot, pl.ds(piece, PIECE)],
                        out.at[pl.ds(piece, PIECE), 2 * first + slot],
                        sems.at[len(copies)],
                    )
                )
                copies[-1].start()
    for copy in copies:
        copy.wait()


def gram(rep, own, other, first, extra, count, total_frames):
    inputs, wide = own.shape
    slots = 2 * (wide // 128)
    steps = 2 * (other.shape[1] // 128)
    tiles = inputs // 64
    vmem = pl.BlockSpec(memory_space=pltpu.VMEM)
    hbm = pl.BlockSpec(memory_space=pltpu.HBM)
    specs = [pl.BlockSpec(memory_space=pltpu.SMEM), vmem, vmem]
    out_specs = [hbm]
    out_shape = [jax.ShapeDtypeStruct((count, slots, tiles, 128), jnp.bfloat16)]
    scratch = []
    if extra:
        specs.append(hbm)
    if len(extra) > 1:
        specs += [vmem, vmem]
        out_specs.append(hbm)
        out_shape.append(jax.ShapeDtypeStruct(extra[1].shape, jnp.float32))
        scratch.append(pltpu.VMEM(extra[1].shape, jnp.float32))
    return pl.pallas_call(
        lambda *refs: gram_kernel(1.0 / total_frames, first, *refs),
        in_specs=specs,
        out_specs=out_specs,
        out_shape=out_shape,
        scratch_shapes=scratch
        + [
            pltpu.VMEM(((2 * count + 8) * (tiles + 1), 128), jnp.float32),
            pltpu.VMEM((steps, count, tiles, 128), jnp.bfloat16),
            pltpu.SemaphoreType.DMA((1 + steps * (count // PIECE),)),
        ],
        input_output_aliases={3: 0} if extra else {},
        compiler_params=pltpu.CompilerParams(vmem_limit_bytes=VMEM),
        cost_estimate=pl.CostEstimate(
            flops=4 * steps * count * inputs * 256, bytes_accessed=steps << 20, transcendentals=0
        ),
        name="gram",
    )(rep, own, other, *extra)


def on_device(voltages, pfb_window, channel_map, beam_layout):
    feed_count = lax.axis_size("feed")
    rep_count = lax.axis_size("rep")
    inp_dev, own_samples = voltages.shape
    total_frames = own_samples // DFT * rep_count
    inputs = inp_dev * feed_count
    slots = 2 * CHANNELS // feed_count
    swap = [(0, 1), (1, 0)]
    margin = lax.ppermute(voltages[:, own_samples - (TAPS - 1) * DFT :], "rep", [(0, 1)])
    outgoing = filtered(
        voltages, margin, pfb_window.reshape(1, -1), channel_map.reshape(1, -1), feed_count
    )
    own = lax.all_to_all(outgoing, "feed", split_axis=0, concat_axis=0, tiled=True)
    beam_own = beams(own, beam_layout.reshape(1, -1), 1.0 / (total_frames * CYL * POS))
    others, at = [], 0
    for part in PARTS:
        source = own if at + part < slots // 2 else lax.optimization_barrier((own, beam_own))[0]
        others.append(lax.ppermute(source[:, at * 128 : (at + part) * 128], "rep", swap))
        at += part
    beam_other = lax.ppermute(beam_own, "rep", swap)
    rep = lax.axis_index("rep").reshape(1)
    count = inputs // 2 // rep_count
    held, first = (), 0
    for part, other in zip(PARTS, others):
        if first + part == slots // 2:
            held += (beam_own, beam_other)
        held = tuple(gram(rep, own, other, first, held, count, total_frames))
        first += part
    summed, beam_power = held
    tiles = inputs // 128
    visibilities = summed.reshape(count, slots, tiles, 2, 128).transpose(0, 1, 3, 2, 4)
    return visibilities.reshape(count, slots, 2, inputs), beam_power


def solution(mesh):
    return jax.shard_map(
        on_device,
        mesh=mesh,
        in_specs=(P("feed", "rep"), P(), P(), P()),
        out_specs=(P("rep", "feed", None, None), P("feed", None)),
        check_vma=False,
    )
```

```python
import math

import jax
import jax.numpy as jnp
import numpy as np
from jax import lax
from jax.experimental import pallas as pl
from jax.experimental.pallas import tpu as pltpu
from jax.sharding import PartitionSpec as P

CYL = 4
POS = 128
DFT = 2048
CHANNELS = 512
CH0 = 256
TAPS = 4
HALF = DFT // 2
VMEM = 24 * 1024 * 1024
GROUPS = 4
PIECE = 64
HEAD = 4
PARTS = (2, 1, 1)
NT = (((1,), (1,)), ((), ()))


def wave_columns():
    samples = np.arange(HALF)
    tables = []
    for parity in range(2):
        bins = CH0 + np.arange(parity, CHANNELS, 2)
        angles = (samples[:, None] * bins[None, :] % DFT) * (2.0 * np.pi / DFT)
        tables.append(np.concatenate([np.cos(angles), -np.sin(angles)], axis=1))
    return np.stack(tables).astype(np.float32).astype(jnp.bfloat16)


def position_tables():
    places = np.arange(POS)
    angles = (places[:, None] * places[None, :] % POS) * (2.0 * np.pi / POS)
    tables = np.concatenate([np.cos(angles), np.sin(angles)])
    return tables.astype(np.float32).astype(jnp.bfloat16)


def tap_sums(window, volt_of, blocks, frames, first, last):
    inputs = blocks.shape[1] // frames

    def chunk(j, carry):
        low = pl.multiple_of(j * 128, 128)
        sums = []
        for at in (low, pl.multiple_of(low + HALF, 128)):
            weights = [
                jnp.broadcast_to(window[:, pl.ds(t * DFT + at, 128)], (inputs, 128))
                for t in range(TAPS)
            ]
            held = [volt_of(first + t + 1 - TAPS, at) for t in range(TAPS - 1)]
            column = []
            for f in range(first, last):
                held.append(volt_of(f, at))
                total = None
                for t in range(TAPS):
                    if held[t] is not None:
                        term = held[t] * weights[t]
                        total = term if total is None else total + term
                held = held[1:]
                column.append(total)
            sums.append(column)
        for f in range(0, last - first, 2):
            for parity in range(2):
                pair = []
                for k in (f, f + 1):
                    low_sum, high_sum = sums[0][k], sums[1][k]
                    pair.append(low_sum - high_sum if parity else low_sum + high_sum)
                at = (first + f) * inputs
                blocks[parity, at : at + 2 * inputs, pl.ds(low, 128)] = jnp.concatenate(
                    pair, axis=0
                ).astype(jnp.bfloat16)
        return carry

    lax.fori_loop(0, HALF // 128, chunk, 0)


def sums_kernel(
    chans, volt_hbm, window_hbm, slots_hbm, waves_hbm,
    blocks, pick, head, window, waves, order, volt, slots, sems,
):
    inputs = volt.shape[0]
    frames = volt.shape[1] // DFT
    dests = pick.shape[0] // chans
    group = frames // GROUPS
    span = group * DFT
    copies = [
        pltpu.make_async_copy(slots_hbm, slots, sems.at[GROUPS]),
        pltpu.make_async_copy(window_hbm, window, sems.at[GROUPS + 1]),
    ]
    for g in range(GROUPS):
        copies.append(
            pltpu.make_async_copy(
                volt_hbm.at[:, pl.ds(g * span, span)], volt.at[:, pl.ds(g * span, span)], sems.at[g]
            )
        )
    copies.append(pltpu.make_async_copy(waves_hbm, waves, sems.at[GROUPS + 2]))
    for copy in copies:
        copy.start()

    half_ch = CHANNELS // 2
    place = lax.broadcasted_iota(jnp.int32, (dests, CHANNELS), 1)
    channel = jnp.where(place < half_ch, 2 * place, 2 * (place - half_ch) + 1)
    dest = lax.broadcasted_iota(jnp.int32, (dests, CHANNELS), 0)
    copies[0].wait()
    held_by = slots[...].astype(jnp.float32)
    for c in range(chans):
        wanted = jnp.sum(
            jnp.where(place == dest * chans + c, held_by, 0.0), axis=1, keepdims=True
        ).astype(jnp.int32)
        pick[c * dests : (c + 1) * dests, :] = (
            (channel == wanted).astype(jnp.float32).astype(jnp.bfloat16)
        )
    row = lax.broadcasted_iota(jnp.int32, order.shape, 0)
    column = lax.broadcasted_iota(jnp.int32, order.shape, 1)
    source = (row % frames) * inputs + row // frames
    order[...] = (column == source).astype(jnp.float32).astype(jnp.bfloat16)
    copies[1].wait()
    window[...] = window[...] * (1.0 / math.sqrt(TAPS * CHANNELS))

    def volt_of(f, at):
        return None if f < 0 else volt[:, pl.ds(f * DFT + at, 128)].astype(jnp.float32)

    for g in range(GROUPS):
        copies[2 + g].wait()
        tap_sums(window, volt_of, blocks, frames, g * group, (g + 1) * group)
    head[...] = volt[:, : head.shape[1]]
    for copy in copies[2 + GROUPS :]:
        copy.wait()


def spectra_kernel(
    blocks, margin, head, window, pick, waves, order, out, first, spectra, sorted_, rows
):
    inputs = head.shape[0]
    columns = blocks.shape[1]
    frames = columns // inputs
    dests = out.shape[0] // inputs
    chans = pick.shape[0] // dests
    half_ch = CHANNELS // 2

    def volt_of(f, at):
        source, f = (margin, f + TAPS - 1) if f < 0 else (head, f)
        return source[:, pl.ds(f * DFT + at, 128)].astype(jnp.float32)

    tap_sums(window, volt_of, first, HEAD, 0, HEAD)
    for parity in range(2):
        sums = jnp.concatenate([first[parity], blocks[parity, HEAD * inputs :, :]], axis=0)
        spectra[:, parity * CHANNELS : (parity + 1) * CHANNELS] = jnp.dot(
            sums, waves[parity], preferred_element_type=jnp.float32
        ).astype(jnp.bfloat16)
    for parity in range(2):
        turned = jnp.dot(
            order[...],
            spectra[:, parity * CHANNELS : (parity + 1) * CHANNELS],
            preferred_element_type=jnp.float32,
        ).astype(jnp.bfloat16)
        for part in range(2):
            for i in range(inputs):
                to = (2 * i + part) * frames
                sorted_[to : to + frames, parity * half_ch : (parity + 1) * half_ch] = turned[
                    i * frames : (i + 1) * frames, part * half_ch : (part + 1) * half_ch
                ]
    wide = 2 * frames
    pitch = inputs + 1
    for pair in range(0, inputs, 2):
        picked = lax.dot_general(
            pick[...],
            sorted_[pair * wide : (pair + 2) * wide, :],
            NT,
            preferred_element_type=jnp.float32,
        )
        for c in range(chans):
            for i in range(2):
                rows[pl.ds(c * dests * pitch + pair + i, dests, stride=pitch), :] = picked[
                    c * dests : (c + 1) * dests, i * wide : (i + 1) * wide
                ]
    for c in range(chans):
        for dest in range(0, dests, 2):
            at = (c * dests + dest) * pitch
            pair = [rows[at + k * pitch : at + k * pitch + inputs, :] for k in range(2)]
            out[dest * inputs : (dest + 2) * inputs, c * wide : (c + 1) * wide] = jnp.concatenate(
                pair, axis=0
            ).astype(jnp.bfloat16)


def tap_blocks(volt, window, slots, dests):
    inputs, own = volt.shape
    chans = slots.shape[1] // dests
    vmem = pl.BlockSpec(memory_space=pltpu.VMEM)
    hbm = pl.BlockSpec(memory_space=pltpu.HBM)
    waves = jnp.asarray(wave_columns())
    return pl.pallas_call(
        lambda *refs: sums_kernel(chans, *refs),
        in_specs=[hbm] * 4,
        out_specs=[vmem] * 6,
        out_shape=[
            jax.ShapeDtypeStruct((2, inputs * own // DFT, HALF), jnp.bfloat16),
            jax.ShapeDtypeStruct((chans * dests, CHANNELS), jnp.bfloat16),
            jax.ShapeDtypeStruct((inputs, HEAD * DFT), jnp.bfloat16),
            jax.ShapeDtypeStruct(window.shape, jnp.float32),
            jax.ShapeDtypeStruct(waves.shape, jnp.bfloat16),
            jax.ShapeDtypeStruct((inputs * own // DFT,) * 2, jnp.bfloat16),
        ],
        scratch_shapes=[
            pltpu.VMEM(volt.shape, jnp.bfloat16),
            pltpu.VMEM(slots.shape, jnp.int32),
            pltpu.SemaphoreType.DMA((GROUPS + 3,)),
        ],
        compiler_params=pltpu.CompilerParams(vmem_limit_bytes=VMEM),
        cost_estimate=pl.CostEstimate(
            flops=2 * inputs * own * TAPS, bytes_accessed=8 << 20, transcendentals=0
        ),
        name="tap_sums",
    )(*(pltpu.with_memory_space_constraint(x, pltpu.HBM) for x in (volt, window, slots, waves)))


def filtered(volt, margin, window, slots, dests):
    inputs, own = volt.shape
    frames = own // DFT
    chans = slots.shape[1] // dests
    columns = inputs * frames
    vmem = pl.BlockSpec(memory_space=pltpu.VMEM)
    blocks, pick, head, taps, waves, order = tap_blocks(volt, window, slots, dests)
    return pl.pallas_call(
        spectra_kernel,
        in_specs=[vmem] * 7,
        out_specs=vmem,
        out_shape=jax.ShapeDtypeStruct((dests * inputs, chans * 2 * frames), jnp.bfloat16),
        scratch_shapes=[
            pltpu.VMEM((2, HEAD * inputs, HALF), jnp.bfloat16),
            pltpu.VMEM((columns, 2 * CHANNELS), jnp.bfloat16),
            pltpu.VMEM((2 * columns, CHANNELS), jnp.bfloat16),
            pltpu.VMEM(((chans * dests + 8) * (inputs + 1), 2 * frames), jnp.float32),
        ],
        compiler_params=pltpu.CompilerParams(vmem_limit_bytes=VMEM),
        cost_estimate=pl.CostEstimate(
            flops=2 * columns * CHANNELS * 4 * 1024, bytes_accessed=8 << 20, transcendentals=0
        ),
        name="spectra",
    )(blocks, margin, head, taps, pick, waves, order)


def beam_kernel(scale, own, layout, tables, out, mixer, mixed):
    inputs = own.shape[0]
    chans = own.shape[1] // 128
    half = CYL * POS
    lane = lax.broadcasted_iota(jnp.int32, (POS, 128), 1)
    first = lane < 64
    collected = jnp.zeros((POS, 128), jnp.float32)
    feed = lax.broadcasted_iota(jnp.int32, (inputs, POS), 0)
    for h in range(2):
        for y in range(CYL):
            at = h * half + y * POS
            hit = (feed == layout[:, at : at + POS]).astype(jnp.float32).astype(jnp.bfloat16)
            mixer[y * 2 * POS : (y + 1) * 2 * POS, :] = lax.dot_general(
                tables[...], hit, NT, preferred_element_type=jnp.float32
            ).astype(jnp.bfloat16)
        mixed[...] = jnp.dot(mixer[...], own[...], preferred_element_type=jnp.float32)

        def turned(value):
            other = pltpu.roll(value, 64, 1)
            return jnp.where(first, other, -other)

        for c in range(chans):
            at = c * 128
            north = []
            for y in range(CYL):
                base = y * 2 * POS
                cosine = mixed[base : base + POS, at : at + 128]
                sine = mixed[base + POS : base + 2 * POS, at : at + 128]
                north.append(cosine + turned(sine))
            even, odd = north[0] + north[2], north[1] + north[3]
            gap, step = north[0] - north[2], turned(north[1] - north[3])
            easts = [even + odd, gap + step, even - odd, gap - step]
            for e, east in enumerate(easts):
                power = jnp.sum(east * east, axis=1, keepdims=True)
                collected = jnp.where(lane == e * 2 * chans + c * 2 + h, power, collected)
    turned_over = collected.T
    for e in range(CYL):
        out[:, e * POS : (e + 1) * POS] = turned_over[e * 2 * chans : (e + 1) * 2 * chans, :] * scale


def beams(own, layout, scale):
    inputs, wide = own.shape
    chans = wide // 128
    return pl.pallas_call(
        lambda *refs: beam_kernel(scale, *refs),
        out_shape=jax.ShapeDtypeStruct((2 * chans, CYL * POS), jnp.float32),
        scratch_shapes=[
            pltpu.VMEM((CYL * 2 * POS, inputs), jnp.bfloat16),
            pltpu.VMEM((CYL * 2 * POS, wide), jnp.float32),
        ],
        compiler_params=pltpu.CompilerParams(vmem_limit_bytes=VMEM),
        cost_estimate=pl.CostEstimate(
            flops=4 * 1024 * inputs * wide, bytes_accessed=4 << 20, transcendentals=0
        ),
        name="beams",
    )(own, layout, position_tables())


def gram_kernel(scale, first, rep, own, other, *refs):
    out, rows, stage, sems = refs[-4:]
    copies = []
    if len(refs) > 5:
        beam_own, beam_other, out, beam_out, beam, rows, stage, sems = refs[-8:]
        beam[...] = beam_own[...] + beam_other[...]
        copies.append(pltpu.make_async_copy(beam, beam_out, sems.at[0]))
        copies[0].start()
    count, _, tiles, _ = out.shape
    inputs = own.shape[0]
    pitch = tiles + 1
    lane = lax.broadcasted_iota(jnp.int32, (count, 128), 1)
    for c in range(other.shape[1] // 128):
        mine = pl.ds((first + c) * 128, 128)
        theirs = pl.ds(c * 128, 128)
        for half in range(2):
            start = pl.multiple_of(half * (inputs // 2) + rep[0] * count, count)
            plain, turned = [], []
            for part in (own[pl.ds(start, count), mine], other[pl.ds(start, count), theirs]):
                plain.append(part)
                swapped = pltpu.roll(part.astype(jnp.float32), 64, 1)
                turned.append(jnp.where(lane < 64, swapped, -swapped).astype(jnp.bfloat16))
            left = jnp.concatenate(
                [jnp.concatenate(plain, axis=1), jnp.concatenate(turned, axis=1)], axis=0
            )
            base = half * count * pitch
            for at in range(0, inputs, 256):
                right = jnp.concatenate(
                    [own[at : at + 256, mine], other[at : at + 256, theirs]], axis=1
                )
                products = lax.dot_general(left, right, NT, preferred_element_type=jnp.float32)
                for part in range(2):
                    for tile in range(2):
                        to = base + (at // 128 + tile) * 2 + part
                        rows[pl.ds(to, count, stride=pitch), :] = products[
                            part * count : (part + 1) * count, tile * 128 : (tile + 1) * 128
                        ]
            slot = 2 * c + half
            for piece in range(0, count, PIECE):
                for r in range(piece, piece + PIECE):
                    at = base + r * pitch
                    stage[slot, r] = (rows[at : at + tiles, :] * scale).astype(jnp.bfloat16)
                copies.append(
                    pltpu.make_async_copy(
                        stage.at[slot, pl.ds(piece, PIECE)],
                        out.at[pl.ds(piece, PIECE), 2 * first + slot],
                        sems.at[len(copies)],
                    )
                )
                copies[-1].start()
    for copy in copies:
        copy.wait()


def gram(rep, own, other, first, extra, count, total_frames):
    inputs, wide = own.shape
    slots = 2 * (wide // 128)
    steps = 2 * (other.shape[1] // 128)
    tiles = inputs // 64
    vmem = pl.BlockSpec(memory_space=pltpu.VMEM)
    hbm = pl.BlockSpec(memory_space=pltpu.HBM)
    specs = [pl.BlockSpec(memory_space=pltpu.SMEM), vmem, vmem]
    out_specs = [hbm]
    out_shape = [jax.ShapeDtypeStruct((count, slots, tiles, 128), jnp.bfloat16)]
    scratch = []
    if extra:
        specs.append(hbm)
    if len(extra) > 1:
        specs += [vmem, vmem]
        out_specs.append(hbm)
        out_shape.append(jax.ShapeDtypeStruct(extra[1].shape, jnp.float32))
        scratch.append(pltpu.VMEM(extra[1].shape, jnp.float32))
    return pl.pallas_call(
        lambda *refs: gram_kernel(1.0 / total_frames, first, *refs),
        in_specs=specs,
        out_specs=out_specs,
        out_shape=out_shape,
        scratch_shapes=scratch
        + [
            pltpu.VMEM(((2 * count + 8) * (tiles + 1), 128), jnp.float32),
            pltpu.VMEM((steps, count, tiles, 128), jnp.bfloat16),
            pltpu.SemaphoreType.DMA((1 + steps * (count // PIECE),)),
        ],
        input_output_aliases={3: 0} if extra else {},
        compiler_params=pltpu.CompilerParams(vmem_limit_bytes=VMEM),
        cost_estimate=pl.CostEstimate(
            flops=4 * steps * count * inputs * 256, bytes_accessed=steps << 20, transcendentals=0
        ),
        name="gram",
    )(rep, own, other, *extra)


def on_device(voltages, pfb_window, channel_map, beam_layout):
    feed_count = lax.axis_size("feed")
    rep_count = lax.axis_size("rep")
    inp_dev, own_samples = voltages.shape
    total_frames = own_samples // DFT * rep_count
    inputs = inp_dev * feed_count
    slots = 2 * CHANNELS // feed_count
    swap = [(0, 1), (1, 0)]
    margin = lax.ppermute(voltages[:, own_samples - (TAPS - 1) * DFT :], "rep", [(0, 1)])
    outgoing = filtered(
        voltages, margin, pfb_window.reshape(1, -1), channel_map.reshape(1, -1), feed_count
    )
    own = lax.all_to_all(outgoing, "feed", split_axis=0, concat_axis=0, tiled=True)
    beam_own = beams(own, beam_layout.reshape(1, -1), 1.0 / (total_frames * CYL * POS))
    others, at = [], 0
    for part in PARTS:
        source = own if at + part < slots // 2 else lax.optimization_barrier((own, beam_own))[0]
        others.append(lax.ppermute(source[:, at * 128 : (at + part) * 128], "rep", swap))
        at += part
    beam_other = lax.ppermute(beam_own, "rep", swap)
    rep = lax.axis_index("rep").reshape(1)
    count = inputs // 2 // rep_count
    held, first = (), 0
    for part, other in zip(PARTS, others):
        if first + part == slots // 2:
            held += (beam_own, beam_other)
        held = tuple(gram(rep, own, other, first, held, count, total_frames))
        first += part
    summed, beam_power = held
    tiles = inputs // 128
    visibilities = summed.reshape(count, slots, tiles, 2, 128).transpose(0, 1, 3, 2, 4)
    return visibilities.reshape(count, slots, 2, inputs), beam_power


def solution(mesh):
    return jax.shard_map(
        on_device,
        mesh=mesh,
        in_specs=(P("feed", "rep"), P(), P(), P()),
        out_specs=(P("rep", "feed", None, None), P("feed", None)),
        check_vma=False,
    )
```
